256 devices in a mesh: lat: 64 (over y, x, z_hi, core), grp: 4 (over z_lo).
Axes of the slice: x: 4, y: 4, z: 8 (z_hi: 2, z_lo: 4; z = z_hi * 4 + z_lo), core: 2. Of those that a mesh axis runs over, the one named last changes fastest.
Arguments:
- increments: bfloat16 [16384, 4, 16, 128], P(('lat', 'grp')), may hold values from -6 to 6
- band: int32 [16384, 1], P(('lat', 'grp')), may hold values from 0 to 63; in each aligned block of 64 rows (0 to 63, 64 to 127, ...) at most 3 rows name the same one
- tile_index: int32 [16384], P(('lat', 'grp')), may hold values from 0 to 7
- lat_offset: int32 [16384], P(('lat', 'grp')), may hold values from 0 to 12
- lon_shift: int32 [16384], P(('lat', 'grp')), may hold values from -8 to 8
- lat_frac: float32 [16384], P(('lat', 'grp')), may hold values from 0 to 1
- lon_frac: float32 [16384, 128], P(('lat', 'grp')), may hold values from 0 to 1
Outputs:
- source_adjoint: float32 [16, 4, 8192, 128], P('grp', None, 'lat')
The draws below stay inside these ranges and needn't reach their ends.
Inputs may be any that keep to these rules, and one draw needn't show every extreme that they name: In the rows of one device no band is named more than 3 times, a bound that some block reaches.
All inputs are finite; a program needn't handle non-finite values.
Results may differ from the reference program's by a relative error of at most 0.0045.
Values may be sent and summed in bfloat16 or wider, within the bound.
No kernel may reach another device: no remote copies, remote signals or barrier semaphores. Data moves between devices by JAX's collectives and lax.ppermute only.
A program may use at most 64 MiB of HBM per device.

```python
import math
import jax
import jax.numpy as jnp
import numpy as np
from jax import lax

F = 4
L = 16
POINTS = 128
TL = 16
TILES_DEV = 8
ROWS_DEV = 64
CAP = 3
ROWS = 16384
TILE_ROWS = 8192
N_LAT = 64


def place_ends(array, stream_key, low, top_value):
    dims = array.shape
    spot = [jax.random.randint(jax.random.fold_in(stream_key, axis), (), 0, dims[axis]) for axis in range(len(dims))]
    array = array.at[tuple(spot)].set(low)
    longest = dims.index(max(dims))
    spot[longest] = (spot[longest] + 1) % dims[longest]
    return array.at[tuple(spot)].set(top_value)


def level_of(rng, dims, split, low, high):
    level, own = 1.0, jax.random.fold_in(rng, 6)
    for axis_at, blocks in split:
        draws = jnp.exp(jax.random.uniform(jax.random.fold_in(own, axis_at), (blocks,), jnp.float32, low / len(split), high / len(split)))
        level = level * jnp.repeat(draws, dims[axis_at] // blocks).reshape([-1 if axis == axis_at else 1 for axis in range(len(dims))])
    return level


def deal_out(key, own, number, rows, amount, top, reach, skew):
    order = jax.random.permutation(key, amount)
    heavy_load, common = shares(amount, rows * top, reach, skew, True), shares(amount, rows * top, reach, skew, False)
    places = jnp.arange(amount)

    def named(lengths, rotation):
        used = int((lengths > 0).sum())
        fixed = max(1, used // 4)
        shifted = fixed + (places - fixed + rotation * (used - fixed)) % max(1, amount - fixed)
        return jnp.zeros((amount,), jnp.int32).at[order[jnp.where(places < fixed, places, shifted)]].set(jnp.asarray(lengths, jnp.int32))

    lengths = jnp.where(number % 4 == 0, named(heavy_load, number // 4), named(common, number - number // 4 - 1))
    mixed = jax.random.permutation(jax.random.fold_in(own, 3), amount)
    giver, taker = mixed[0:amount // 2 * 2:2], mixed[1:amount // 2 * 2:2]
    room = jnp.minimum(lengths[giver] - 1, reach - lengths[taker]) // 2
    room = jnp.where((giver == order[0]) | (taker == order[0]) | (lengths[taker] == 0), 0, jnp.maximum(room, 0))
    shifted = jax.random.randint(jax.random.fold_in(own, 4), (amount // 2,), 0, 1 << 20) % (room + 1)
    lengths = lengths.at[giver].add(-shifted).at[taker].add(shifted)
    members = jnp.searchsorted(jnp.cumsum(lengths), jnp.arange(rows * top), side="right").astype(jnp.int32)
    grid = members.reshape(top, rows).T
    grid = grid[jax.random.permutation(jax.random.fold_in(own, 1), rows)]
    rotation = jax.random.randint(jax.random.fold_in(own, 2), (rows, 1), 0, top)
    return jnp.take_along_axis(grid, (jnp.arange(top)[None, :] + rotation) % top, axis=1)


def shares(amount, total, limit, skew, full):
    portions = [(1 << 20) // math.isqrt(grade ** skew) + 1 for grade in range(1, amount + 1)]
    largest = limit if full else min(limit, max(-(-total // amount), total * portions[0] // sum(portions)))
    least = 1 if total - largest >= amount - 1 else 0
    counts, rest = [largest] + [least] * (amount - 1), total - largest - least * (amount - 1)
    while rest > 0:
        movable = [i for i in range(1, amount) if counts[i] < largest] or [i for i in range(1, amount) if counts[i] < limit]
        whole, left = sum([portions[i] for i in movable]), rest
        for i in movable:
            more = min(limit - counts[i], max(1, left * portions[i] // whole), rest)
            counts[i] = counts[i] + more
            rest = rest - more
    return np.array(counts)


def noise(own_key, dims, deviation, limit, pieces=(), held_as=jnp.bfloat16):
    result = deviation * jax.random.normal(own_key, dims, jnp.float32)
    if pieces:
        result = result * level_of(own_key, dims, pieces, -0.22, 0.18)
    return jnp.clip(result, -limit, limit).astype(held_as)


def setup_inputs(seed: int = 0) -> dict:
    arg_keys = jax.random.split(jax.random.key(seed), 8)
    increments = noise(arg_keys[0], (ROWS, F, L, POINTS), 1.0, 6.0, ((0, 256),))
    band_keys = jax.random.split(jax.random.fold_in(arg_keys[1], 1), ROWS // ROWS_DEV)
    band_turns = jax.random.permutation(jax.random.fold_in(arg_keys[1], 3), ROWS // ROWS_DEV)
    band = jax.vmap(lambda own, number: deal_out(jax.random.fold_in(arg_keys[1], 2), own, number, ROWS_DEV, N_LAT, 1, CAP, 2))(band_keys, band_turns).reshape((ROWS, 1))
    tile_index = place_ends(jax.random.randint(arg_keys[2], (ROWS,), 0, TILES_DEV), jax.random.fold_in(arg_keys[2], 1), 0, TILES_DEV - 1).astype(jnp.int32)
    lat_offset = place_ends(jax.random.randint(arg_keys[3], (ROWS,), 0, TL - 3), jax.random.fold_in(arg_keys[3], 1), 0, (TL - 3) - 1).astype(jnp.int32)
    lon_shift = place_ends(jax.random.randint(arg_keys[4], (ROWS,), -8, 9), jax.random.fold_in(arg_keys[4], 1), -8, 8).astype(jnp.int32)
    lat_frac = jnp.clip(1.0 * jax.random.uniform(arg_keys[5], (ROWS,), jnp.float32) ** level_of(arg_keys[5], (ROWS,), ((0, 256),), -0.2, 0.2), 0.0, 1.0)
    lon_frac = jnp.clip(1.0 * jax.random.uniform(arg_keys[6], (ROWS, POINTS), jnp.float32) ** level_of(arg_keys[6], (ROWS, POINTS), ((0, 256),), -0.2, 0.2), 0.0, 1.0)
    return dict(increments=increments, band=band, tile_index=tile_index, lat_offset=lat_offset, lon_shift=lon_shift, lat_frac=lat_frac, lon_frac=lon_frac)


def lagrange(fraction):
    return [-fraction * (fraction - 1.0) * (fraction - 2.0) / 6.0,
            (fraction + 1.0) * (fraction - 1.0) * (fraction - 2.0) / 2.0,
            -(fraction + 1.0) * fraction * (fraction - 2.0) / 2.0,
            (fraction + 1.0) * fraction * (fraction - 1.0) / 6.0]


def reference(increments, band, tile_index, lat_offset, lon_shift, lat_frac, lon_frac):
    row_count = increments.shape[0]
    width = math.gcd(row_count, 512)
    lon_weight = [w.astype(jnp.bfloat16) for w in lagrange(lon_frac)]
    lat_weight = [w.astype(jnp.bfloat16) for w in lagrange(lat_frac)]
    band_base = band[:, 0] * (TILES_DEV * TL) + lat_offset
    here_rows = (band_base + tile_index * TL).astype(jnp.int32)
    next_rows = (band_base + ((tile_index + 1) % TILES_DEV) * TL).astype(jnp.int32)
    prev_rows = (band_base + ((tile_index + TILES_DEV - 1) % TILES_DEV) * TL).astype(jnp.int32)
    columns = jnp.arange(POINTS, dtype=jnp.int32)
    low_half = (columns < POINTS // 2)[None, None, None, :]

    def one_block(total, number):
        first = (number * width).astype(jnp.int32)
        values = lax.dynamic_slice_in_dim(increments, first, width, 0).astype(jnp.float32)
        shifts = lax.dynamic_slice_in_dim(lon_shift, first, width, 0)
        own = jnp.zeros(values.shape, jnp.float32)
        spill = jnp.zeros(values.shape, jnp.float32)
        for m in range(4):
            weight = lax.dynamic_slice_in_dim(lon_weight[m], first, width, 0).astype(jnp.float32)
            scaled = values * weight[:, None, None, :]
            raw = (columns[None, :] - shifts[:, None] - m + 1).astype(jnp.int32)
            inside = (raw >= 0) & (raw < POINTS)
            source = (raw % POINTS).astype(jnp.int32)
            source = jnp.broadcast_to(source[:, None, None, :], scaled.shape)
            picked = jnp.take_along_axis(scaled, source, axis=3)
            inside = inside[:, None, None, :]
            own = own + jnp.where(inside, picked, 0.0)
            spill = spill + jnp.where(inside, 0.0, picked)
        own = lax.optimization_barrier(own.astype(jnp.bfloat16)).astype(jnp.float32)
        spill = lax.optimization_barrier(spill.astype(jnp.bfloat16)).astype(jnp.float32)
        spill_next = jnp.where(low_half, spill, 0.0)
        spill_prev = jnp.where(low_half, 0.0, spill)
        rows_here = lax.dynamic_slice_in_dim(here_rows, first, width, 0)
        rows_next = lax.dynamic_slice_in_dim(next_rows, first, width, 0)
        rows_prev = lax.dynamic_slice_in_dim(prev_rows, first, width, 0)
        for k in range(4):
            weight = lax.dynamic_slice_in_dim(lat_weight[k], first, width, 0).astype(jnp.float32)[:, None, None, None]
            total = total.at[rows_here + k].add(weight * own)
            total = total.at[rows_next + k].add(weight * spill_next)
            total = total.at[rows_prev + k].add(weight * spill_prev)
        return total, None

    total = jnp.zeros((TILE_ROWS, F, L, POINTS), jnp.float32)
    total, _ = lax.scan(one_block, total, jnp.arange(row_count // width, dtype=jnp.int32))
    return jnp.transpose(total, (2, 1, 0, 3))
```

```python
import jax
import jax.numpy as jnp
from jax import lax
from jax.experimental import pallas as pl
from jax.experimental.pallas import tpu as pltpu
from jax.sharding import PartitionSpec as P

TL = 16
CAP = 3
SLOT_ROWS = 16
OWN_ROWS = CAP * SLOT_ROWS
PEER_ROWS = OWN_ROWS + 8
META_ROW = 6


def lagrange(fraction):
    return [
        -fraction * (fraction - 1.0) * (fraction - 2.0) / 6.0,
        (fraction + 1.0) * (fraction - 1.0) * (fraction - 2.0) / 2.0,
        -(fraction + 1.0) * fraction * (fraction - 2.0) / 2.0,
        (fraction + 1.0) * fraction * (fraction - 1.0) / 6.0,
    ]


def rounded(x):
    return x.astype(jnp.bfloat16).astype(jnp.float32)


def source_kernel(
    band, tile_index, lat_offset, lon_shift, lat_frac, inc, lon_frac, out, weights, extra, count
):
    rows = inc.shape[0]
    bands = out.shape[0] // 4
    lane = lax.broadcasted_iota(jnp.int32, (8, 128), 1)
    sub = lax.broadcasted_iota(jnp.int32, (8, 128), 0)
    zero = jnp.zeros((8, 128), jnp.float32)

    for m, w in enumerate(lagrange(lon_frac[...])):
        weights[m] = rounded(w)

    def clear(i, _):
        out[pl.ds(i * 4, 4)] = jnp.zeros((4,) + out.shape[1:], jnp.bfloat16)
        extra[pl.ds(i * 4, 4)] = jnp.zeros((4, 8, 128), jnp.float32)
        count[i] = 0
        return 0

    lax.fori_loop(0, bands, clear, 0)

    def one_row(r, _):
        b = band[r]
        slot = count[b]
        count[b] = slot + 1
        shift = lon_shift[r]
        x = inc[r].astype(jnp.float32)
        half = [[x[f, 8 * h : 8 * h + 8] for h in range(2)] for f in range(4)]
        pieces = []
        for g in range(4):
            h, odd = g // 2, g % 2
            for f in (0, 2):
                first, second = half[f][h], half[f + 1][h]
                if odd:
                    first = pltpu.roll(first, 4, 0)
                else:
                    second = pltpu.roll(second, 4, 0)
                pieces.append(jnp.where(sub < 4, first, second))
        own = [zero] * 8
        spill = [zero] * 8
        for m in range(4):
            move = (shift + (m - 1 + 128)) & 127
            w = jnp.broadcast_to(weights[m, pl.ds(r, 1), :], (8, 128))
            w = pltpu.roll(w, move, 1)
            raw = lane - shift - (m - 1)
            inside = (raw >= 0) & (raw < 128)
            own_w = jnp.where(inside, w, 0.0)
            spill_w = jnp.where(inside, 0.0, w)
            for i in range(8):
                moved = pltpu.roll(pieces[i], move, 1)
                own[i] = own[i] + own_w * moved
                spill[i] = spill[i] + spill_w * moved
        spot = lane - 8 * slot
        lat = lagrange(jnp.full((8, 128), lat_frac[r], jnp.float32))
        first_row = (tile_index[r] * TL + lat_offset[r]).astype(jnp.float32)
        meta = jnp.where(spot == 0, first_row, jnp.where(spot == 1, shift.astype(jnp.float32), 0.0))
        for k in range(4):
            meta = jnp.where(spot == 2 + k, lat[k], meta)
        base = jnp.where(sub == META_ROW, meta, 0.0)
        at = pl.multiple_of(slot * SLOT_ROWS, SLOT_ROWS)
        for g in range(4):
            block = jnp.concatenate([own[2 * g], own[2 * g + 1]], axis=0)
            out[b * 4 + g, pl.ds(at, SLOT_ROWS), :] = block.astype(jnp.bfloat16)
            tile = base
            for h in range(2):
                s = spill[2 * g + h]
                folded = jnp.where(lane < 16, s + pltpu.roll(s, 16, 1), 0.0)
                spread = pltpu.roll(folded, 0, 1, stride=16, stride_axis=0)
                line = jnp.sum(spread, axis=0, keepdims=True)
                tile = jnp.where(sub == 2 * slot + h, line, tile)
            extra[b * 4 + g] = extra[b * 4 + g] + tile
        return 0

    lax.fori_loop(0, rows, one_row, 0)

    def finish(i, _):
        out[pl.ds(i * 4, 4), OWN_ROWS:PEER_ROWS, :] = extra[pl.ds(i * 4, 4)].astype(jnp.bfloat16)
        return 0

    lax.fori_loop(0, bands, finish, 0)


def tile_kernel(got, out, wide, extra):
    peers = got.shape[0]

    def widen(p, _):
        wide[pl.ds(pl.multiple_of(p * OWN_ROWS, 8), OWN_ROWS), :] = got[p, 0:OWN_ROWS, :].astype(jnp.float32)
        extra[pl.ds(pl.multiple_of(p * 8, 8), 8), :] = got[p, OWN_ROWS:PEER_ROWS, :].astype(jnp.float32)
        return 0

    lax.fori_loop(0, peers, widen, 0, unroll=4)

    meta = extra[pl.ds(META_ROW, peers, stride=8), :]
    row_id = lax.broadcasted_iota(jnp.int32, (peers, 128), 1).astype(jnp.float32)
    place = lax.broadcasted_iota(jnp.int32, (peers, 128), 1) % 16
    stencil, spill_next, spill_prev = [], [], []
    for j in range(CAP):
        c = 8 * j
        table = jnp.zeros((peers, 128), jnp.float32)
        first_row = meta[:, c : c + 1]
        for k in range(4):
            table = table + jnp.where(row_id == first_row + float(k), meta[:, c + 2 + k : c + 3 + k], 0.0)
        stencil.append(table.T.astype(jnp.bfloat16))
        shift = meta[:, c + 1 : c + 2]
        forward = (shift > 0.5) | ((shift > -1.5) & (place < 8))
        lines = [extra[pl.ds(2 * j + h, peers, stride=8), :] for h in range(2)]
        spill_next.append(jnp.concatenate([jnp.where(forward, s, 0.0) for s in lines], axis=1).astype(jnp.bfloat16))
        spill_prev.append(jnp.concatenate([jnp.where(forward, 0.0, s) for s in lines], axis=1).astype(jnp.bfloat16))
    columns = jnp.concatenate(stencil, axis=1)

    def product(values):
        return jnp.dot(columns, jnp.concatenate(values, axis=0), preferred_element_type=jnp.float32)

    onward = product(spill_next)
    onward = jnp.concatenate([onward[128 - TL :], onward[: 128 - TL]], axis=0)
    back = product(spill_prev)
    back = jnp.concatenate([back[TL:], back[:TL]], axis=0)
    lane = lax.broadcasted_iota(jnp.int32, (128, 128), 1)
    for pair in range(8):
        values = []
        for j in range(CAP):
            cols = [
                wide[pl.ds(j * SLOT_ROWS + 2 * pair + e, peers, stride=OWN_ROWS), :].astype(jnp.bfloat16)
                for e in range(2)
            ]
            values.append(jnp.concatenate(cols, axis=1))
        total = product(values)
        for e in range(2):
            fl = 2 * pair + e
            h, i = fl // 8, fl % 8
            ahead = pltpu.roll(onward[:, 128 * h : 128 * h + 128], (128 - 16 * i) % 128, 1)
            behind = pltpu.roll(back[:, 128 * h : 128 * h + 128], (112 - 16 * i) % 128, 1)
            edges = jnp.where(lane < 16, ahead, jnp.where(lane >= 112, behind, 0.0))
            out[fl % 4, fl // 4] = total[:, 128 * e : 128 * e + 128] + edges


def local(increments, band, tile_index, lat_offset, lon_shift, lat_frac, lon_frac):
    rows = increments.shape[0]
    n_lat = lax.axis_size("lat")
    peers = 4 * n_lat
    smem = pl.BlockSpec(memory_space=pltpu.SMEM)
    vmem = pl.BlockSpec(memory_space=pltpu.VMEM)
    send = pl.pallas_call(
        source_kernel,
        out_shape=jax.ShapeDtypeStruct((peers, PEER_ROWS, 128), jnp.bfloat16),
        in_specs=[smem] * 5 + [vmem] * 2,
        out_specs=vmem,
        scratch_shapes=[
            pltpu.VMEM((4, rows, 128), jnp.float32),
            pltpu.VMEM((peers, 8, 128), jnp.float32),
            pltpu.SMEM((n_lat,), jnp.int32),
        ],
        compiler_params=pltpu.CompilerParams(vmem_limit_bytes=24 << 20),
        name="lon_slots",
    )(band.reshape(rows), tile_index, lat_offset, lon_shift, lat_frac, increments, lon_frac)
    got = lax.all_to_all(send, ("lat", "grp"), 0, 0, tiled=True)
    return pl.pallas_call(
        tile_kernel,
        out_shape=jax.ShapeDtypeStruct((4, 4, 128, 128), jnp.float32),
        in_specs=[vmem],
        out_specs=vmem,
        scratch_shapes=[
            pltpu.VMEM((peers * OWN_ROWS, 128), jnp.float32),
            pltpu.VMEM((peers * 8, 128), jnp.float32),
        ],
        compiler_params=pltpu.CompilerParams(vmem_limit_bytes=40 << 20),
        name="tile_sums",
    )(got)


def solution(mesh):
    in_specs = (
        P(("lat", "grp"), None, None, None),
        P(("lat", "grp"), None),
        P(("lat", "grp")),
        P(("lat", "grp")),
        P(("lat", "grp")),
        P(("lat", "grp")),
        P(("lat", "grp"), None),
    )
    out_specs = P("grp", None, "lat", None)
    return jax.shard_map(local, mesh=mesh, in_specs=in_specs, out_specs=out_specs, check_vma=False)
```

```python
import jax
import jax.numpy as jnp
from jax import lax
from jax.experimental import pallas as pl
from jax.experimental.pallas import tpu as pltpu
from jax.sharding import PartitionSpec as P

TL = 16
CAP = 3
SLOT_ROWS = 16
OWN_ROWS = CAP * SLOT_ROWS
PEER_ROWS = OWN_ROWS + CAP + 1
EDGE = 10
WHOLE = 12
META = EDGE * WHOLE


def lagrange(fraction):
    return [
        -fraction * (fraction - 1.0) * (fraction - 2.0) / 6.0,
        (fraction + 1.0) * (fraction - 1.0) * (fraction - 2.0) / 2.0,
        -(fraction + 1.0) * fraction * (fraction - 2.0) / 2.0,
        (fraction + 1.0) * fraction * (fraction - 1.0) / 6.0,
    ]


def rounded(x):
    return x.astype(jnp.bfloat16).astype(jnp.float32)


def source_kernel(
    band_hbm, tile_hbm, offset_hbm, shift_hbm, lat_hbm, inc_hbm, lon_hbm, out,
    band, tile_index, lat_offset, lon_shift, lat_frac, count, first, slot_of,
    inc, lon_frac, weights, stage, edges, meta_lines, lines, sems,
):
    rows = inc.shape[0]
    bands = count.shape[0]
    pairs = (
        (band_hbm, band), (tile_hbm, tile_index), (offset_hbm, lat_offset), (shift_hbm, lon_shift),
        (lat_hbm, lat_frac), (lon_hbm, lon_frac), (inc_hbm, inc),
    )
    copies = [pltpu.make_async_copy(src, dst, sems.at[i]) for i, (src, dst) in enumerate(pairs)]
    for copy in copies:
        copy.start()

    lane = lax.broadcasted_iota(jnp.int32, (8, 128), 1)
    sub = lax.broadcasted_iota(jnp.int32, (8, 128), 0)
    zero = jnp.zeros((8, 128), jnp.float32)
    part = stage.shape[0] // bands

    def clear(i, _):
        stage[pl.ds(pl.multiple_of(i * part, 8), part), :] = jnp.zeros((part, 128), jnp.float32)
        count[i] = 0
        return 0

    lax.fori_loop(0, bands, clear, 0)
    for copy in copies:
        copy.wait()

    for m, w in enumerate(lagrange(lon_frac[...])):
        weights[m] = rounded(w)

    def one_row(r, _):
        b = band[r]
        slot = count[b]
        count[b] = slot + 1
        slot_of[r] = slot
        peer_row = b * (4 * PEER_ROWS)
        first[r] = peer_row
        shift = lon_shift[r]
        x = inc[r].astype(jnp.float32)
        half = [[x[f, 8 * h : 8 * h + 8] for h in range(2)] for f in range(4)]
        pieces = []
        for g in range(4):
            h, odd = g // 2, g % 2
            for f in (0, 2):
                upper, lower = half[f][h], half[f + 1][h]
                if odd:
                    upper = pltpu.roll(upper, 4, 0)
                else:
                    lower = pltpu.roll(lower, 4, 0)
                pieces.append(jnp.where(sub < 4, upper, lower))
        own = [None] * 8
        spill = [None] * 8
        for m in range(4):
            move = (shift + (m - 1 + 128)) & 127
            w = jnp.broadcast_to(weights[m, pl.ds(r, 1), :], (8, 128))
            w = pltpu.roll(w, move, 1)
            raw = lane - shift - (m - 1)
            inside = (raw >= 0) & (raw < 128)
            own_w = jnp.where(inside, w, 0.0)
            spill_w = jnp.where(inside, 0.0, w)
            for i in range(8):
                moved = pltpu.roll(pieces[i], move, 1)
                own[i] = own_w * moved if m == 0 else own[i] + own_w * moved
                spill[i] = spill_w * moved if m == 0 else spill[i] + spill_w * moved
        for i in range(8):
            stage[pl.ds(peer_row + (i // 2) * PEER_ROWS + slot * SLOT_ROWS + 8 * (i % 2), 8), :] = own[i]
            folded = jnp.where(lane < EDGE, spill[i] + pltpu.roll(spill[i], EDGE, 1), 0.0)
            edges[pl.ds(pl.multiple_of(r * 64 + 8 * i, 8), 8), :] = folded
        lat = lagrange(jnp.full((8, 128), lat_frac[r], jnp.float32))
        start = (tile_index[r] * TL + lat_offset[r]).astype(jnp.float32)
        meta = jnp.where(lane == META, start, jnp.where(lane == META + 1, shift.astype(jnp.float32), 0.0))
        for k in range(4):
            meta = jnp.where(lane == META + 2 + k, lat[k], meta)
        meta_lines[pl.ds(r, 1), :] = meta[0:1]
        return 0

    lax.fori_loop(0, rows, one_row, 0, unroll=4)

    for g in range(4):
        whole = meta_lines[...]
        rest = None
        for fl in range(SLOT_ROWS):
            line = edges[pl.ds(g * SLOT_ROWS + fl, rows, stride=64), :]
            if fl < WHOLE:
                whole = whole + (pltpu.roll(line, EDGE * fl, 1) if fl else line)
            else:
                line = pltpu.roll(line, EDGE * (fl - WHOLE), 1) if fl > WHOLE else line
                rest = line if rest is None else rest + line
        lines[2 * g] = whole
        lines[2 * g + 1] = rest

    def place(r, _):
        slot = slot_of[r]
        for g in range(4):
            at = first[r] + g * PEER_ROWS + OWN_ROWS
            stage[pl.ds(at + slot, 1), :] = lines[2 * g, pl.ds(r, 1), :]
            rest = jnp.broadcast_to(lines[2 * g + 1, pl.ds(r, 1), :], (8, 128))
            rest = pltpu.roll(rest, slot * (4 * EDGE), 1)
            stage[pl.ds(at + CAP, 1), :] = stage[pl.ds(at + CAP, 1), :] + rest[0:1]
        return 0

    lax.fori_loop(0, rows, place, 0, unroll=4)

    def finish(i, _):
        piece = pl.ds(pl.multiple_of(i * part, 16), part)
        out[piece, :] = stage[piece, :].astype(jnp.bfloat16)
        return 0

    lax.fori_loop(0, bands, finish, 0)


def tile_kernel(got, out, wide):
    peers = got.shape[0] // PEER_ROWS
    part = 4 * PEER_ROWS

    def widen(p, _):
        piece = pl.ds(pl.multiple_of(p * part, 16), part)
        wide[piece, :] = got[piece, :].astype(jnp.float32)
        return 0

    lax.fori_loop(0, peers // 4, widen, 0)

    def line_of_all(row):
        return wide[pl.ds(row, peers, stride=PEER_ROWS), :]

    lanes = lax.broadcasted_iota(jnp.int32, (peers, 128), 1)
    row_id = lanes.astype(jnp.float32)
    place = lanes % EDGE
    shared = line_of_all(OWN_ROWS + CAP)
    stencil, spill_next, spill_prev = [], [], []
    for j in range(CAP):
        line = line_of_all(OWN_ROWS + j)
        table = jnp.zeros((peers, 128), jnp.float32)
        start = line[:, META : META + 1]
        for k in range(4):
            table = table + jnp.where(row_id == start + float(k), line[:, META + 2 + k : META + 3 + k], 0.0)
        stencil.append(table.T.astype(jnp.bfloat16))
        shift = line[:, META + 1 : META + 2]
        forward = (shift > 0.5) | ((shift > -1.5) & (place < EDGE // 2))
        rest = pltpu.roll(shared, (128 - 4 * EDGE * j) % 128, 1) if j else shared
        both = [line, rest]
        spill_next.append(jnp.concatenate([jnp.where(forward, s, 0.0) for s in both], axis=1).astype(jnp.bfloat16))
        spill_prev.append(jnp.concatenate([jnp.where(forward, 0.0, s) for s in both], axis=1).astype(jnp.bfloat16))
    columns = jnp.concatenate(stencil, axis=1)

    def product(values):
        return jnp.dot(columns, jnp.concatenate(values, axis=0), preferred_element_type=jnp.float32)

    onward = product(spill_next)
    onward = jnp.concatenate([onward[128 - TL :], onward[: 128 - TL]], axis=0)
    back = product(spill_prev)
    back = jnp.concatenate([back[TL:], back[:TL]], axis=0)
    lane = lax.broadcasted_iota(jnp.int32, (128, 128), 1)
    for pair in range(8):
        values = []
        for j in range(CAP):
            cols = [line_of_all(j * SLOT_ROWS + 2 * pair + e).astype(jnp.bfloat16) for e in range(2)]
            values.append(jnp.concatenate(cols, axis=1))
        total = product(values)
        for e in range(2):
            fl = 2 * pair + e
            h, i = fl // WHOLE, fl % WHOLE
            ahead = pltpu.roll(onward[:, 128 * h : 128 * h + 128], (128 - EDGE * i) % 128, 1)
            behind = pltpu.roll(back[:, 128 * h : 128 * h + 128], (256 - EDGE - EDGE * i) % 128, 1)
            around = jnp.where(lane < EDGE, ahead, jnp.where(lane >= 128 - EDGE, behind, 0.0))
            out[fl % 4, fl // 4] = total[:, 128 * e : 128 * e + 128] + around


def local(increments, band, tile_index, lat_offset, lon_shift, lat_frac, lon_frac):
    rows = increments.shape[0]
    n_lat = lax.axis_size("lat")
    peers = 4 * n_lat
    hbm = pl.BlockSpec(memory_space=pltpu.HBM)
    vmem = pl.BlockSpec(memory_space=pltpu.VMEM)
    whole = (peers * PEER_ROWS, 128)
    send = pl.pallas_call(
        source_kernel,
        out_shape=jax.ShapeDtypeStruct(whole, jnp.bfloat16),
        in_specs=[hbm] * 7,
        out_specs=vmem,
        scratch_shapes=[pltpu.SMEM((rows,), jnp.int32)] * 4
        + [pltpu.SMEM((rows,), jnp.float32), pltpu.SMEM((n_lat,), jnp.int32)]
        + [pltpu.SMEM((rows,), jnp.int32)] * 2
        + [
            pltpu.VMEM(increments.shape, jnp.bfloat16),
            pltpu.VMEM((rows, 128), jnp.float32),
            pltpu.VMEM((4, rows, 128), jnp.float32),
            pltpu.VMEM(whole, jnp.float32),
            pltpu.VMEM((rows * 64, 128), jnp.float32),
            pltpu.VMEM((rows, 128), jnp.float32),
            pltpu.VMEM((8, rows, 128), jnp.float32),
            pltpu.SemaphoreType.DMA((7,)),
        ],
        compiler_params=pltpu.CompilerParams(vmem_limit_bytes=32 << 20),
        name="lon_slots",
    )(band.reshape(rows), tile_index, lat_offset, lon_shift, lat_frac, increments, lon_frac)
    fine = (peers * PEER_ROWS // 4, 4, 128)
    got = lax.all_to_all(send.reshape(fine), ("lat", "grp"), 0, 0, tiled=True)
    return pl.pallas_call(
        tile_kernel,
        out_shape=jax.ShapeDtypeStruct((4, 4, 128, 128), jnp.float32),
        in_specs=[vmem],
        out_specs=vmem,
        scratch_shapes=[pltpu.VMEM(whole, jnp.float32)],
        compiler_params=pltpu.CompilerParams(vmem_limit_bytes=40 << 20),
        name="tile_sums",
    )(got.reshape(whole))


def solution(mesh):
    in_specs = (
        P(("lat", "grp"), None, None, None),
        P(("lat", "grp"), None),
        P(("lat", "grp")),
        P(("lat", "grp")),
        P(("lat", "grp")),
        P(("lat", "grp")),
        P(("lat", "grp"), None),
    )
    out_specs = P("grp", None, "lat", None)
    return jax.shard_map(local, mesh=mesh, in_specs=in_specs, out_specs=out_specs, check_vma=False)
```

```python
import jax
import jax.numpy as jnp
from jax import lax
from jax.experimental import pallas as pl
from jax.experimental.pallas import tpu as pltpu
from jax.sharding import PartitionSpec as P

TL = 16
CAP = 3
SLOT_ROWS = 16
OWN_ROWS = CAP * SLOT_ROWS
PEER_ROWS = OWN_ROWS + CAP + 1
EDGE = 10
WHOLE = 12
META = EDGE * WHOLE


def lagrange(fraction):
    return [
        -fraction * (fraction - 1.0) * (fraction - 2.0) / 6.0,
        (fraction + 1.0) * (fraction - 1.0) * (fraction - 2.0) / 2.0,
        -(fraction + 1.0) * fraction * (fraction - 2.0) / 2.0,
        (fraction + 1.0) * fraction * (fraction - 1.0) / 6.0,
    ]


def rounded(x):
    return x.astype(jnp.bfloat16).astype(jnp.float32)


def source_kernel(
    band_hbm, tile_hbm, offset_hbm, shift_hbm, lat_hbm, inc_hbm, lon_hbm, out,
    band, tile_index, lat_offset, lon_shift, lat_frac, count, first, slot_of,
    inc, lon_frac, weights, stage, edges, meta_lines, lines, sems,
):
    rows = inc.shape[0]
    bands = count.shape[0]
    pairs = (
        (band_hbm, band), (tile_hbm, tile_index), (offset_hbm, lat_offset), (shift_hbm, lon_shift),
        (lat_hbm, lat_frac), (lon_hbm, lon_frac), (inc_hbm, inc),
    )
    copies = [pltpu.make_async_copy(src, dst, sems.at[i]) for i, (src, dst) in enumerate(pairs)]
    for copy in copies:
        copy.start()

    lane = lax.broadcasted_iota(jnp.int32, (8, 128), 1)
    sub = lax.broadcasted_iota(jnp.int32, (8, 128), 0)
    zero = jnp.zeros((8, 128), jnp.float32)
    part = stage.shape[0] // bands

    def clear(i, _):
        stage[pl.ds(pl.multiple_of(i * part, 8), part), :] = jnp.zeros((part, 128), jnp.float32)
        count[i] = 0
        return 0

    lax.fori_loop(0, bands, clear, 0)
    for copy in copies:
        copy.wait()

    for m, w in enumerate(lagrange(lon_frac[...])):
        weights[m] = rounded(w)

    def one_row(r, _):
        b = band[r]
        slot = count[b]
        count[b] = slot + 1
        slot_of[r] = slot
        peer_row = b * (4 * PEER_ROWS)
        first[r] = peer_row
        shift = lon_shift[r]
        x = inc[r].astype(jnp.float32)
        half = [[x[f, 8 * h : 8 * h + 8] for h in range(2)] for f in range(4)]
        pieces = []
        for g in range(4):
            h, odd = g // 2, g % 2
            for f in (0, 2):
                upper, lower = half[f][h], half[f + 1][h]
                if odd:
                    upper = pltpu.roll(upper, 4, 0)
                else:
                    lower = pltpu.roll(lower, 4, 0)
                pieces.append(jnp.where(sub < 4, upper, lower))
        own = [None] * 8
        spill = [None] * 8
        for m in range(4):
            move = (shift + (m - 1 + 128)) & 127
            w = jnp.broadcast_to(weights[m, pl.ds(r, 1), :], (8, 128))
            w = pltpu.roll(w, move, 1)
            raw = lane - shift - (m - 1)
            inside = (raw >= 0) & (raw < 128)
            own_w = jnp.where(inside, w, 0.0)
            spill_w = jnp.where(inside, 0.0, w)
            for i in range(8):
                moved = pltpu.roll(pieces[i], move, 1)
                own[i] = own_w * moved if m == 0 else own[i] + own_w * moved
                spill[i] = spill_w * moved if m == 0 else spill[i] + spill_w * moved
        for i in range(8):
            stage[pl.ds(peer_row + (i // 2) * PEER_ROWS + slot * SLOT_ROWS + 8 * (i % 2), 8), :] = own[i]
            folded = jnp.where(lane < EDGE, spill[i] + pltpu.roll(spill[i], EDGE, 1), 0.0)
            edges[pl.ds(pl.multiple_of(r * 64 + 8 * i, 8), 8), :] = folded
        lat = lagrange(jnp.full((8, 128), lat_frac[r], jnp.float32))
        start = (tile_index[r] * TL + lat_offset[r]).astype(jnp.float32)
        meta = jnp.where(lane == META, start, jnp.where(lane == META + 1, shift.astype(jnp.float32), 0.0))
        for k in range(4):
            meta = jnp.where(lane == META + 2 + k, lat[k], meta)
        meta_lines[pl.ds(r, 1), :] = meta[0:1]
        return 0

    lax.fori_loop(0, rows, one_row, 0, unroll=4)

    for g in range(4):
        whole = meta_lines[...]
        rest = None
        for fl in range(SLOT_ROWS):
            line = edges[pl.ds(g * SLOT_ROWS + fl, rows, stride=64), :]
            if fl < WHOLE:
                whole = whole + (pltpu.roll(line, EDGE * fl, 1) if fl else line)
            else:
                line = pltpu.roll(line, EDGE * (fl - WHOLE), 1) if fl > WHOLE else line
                rest = line if rest is None else rest + line
        lines[2 * g] = whole
        lines[2 * g + 1] = rest

    def place(r, _):
        slot = slot_of[r]
        for g in range(4):
            at = first[r] + g * PEER_ROWS + OWN_ROWS
            stage[pl.ds(at + slot, 1), :] = lines[2 * g, pl.ds(r, 1), :]
            rest = jnp.broadcast_to(lines[2 * g + 1, pl.ds(r, 1), :], (8, 128))
            rest = pltpu.roll(rest, slot * (4 * EDGE), 1)
            stage[pl.ds(at + CAP, 1), :] = stage[pl.ds(at + CAP, 1), :] + rest[0:1]
        return 0

    lax.fori_loop(0, rows, place, 0, unroll=4)

    def finish(i, _):
        piece = pl.ds(pl.multiple_of(i * part, 16), part)
        out[piece, :] = stage[piece, :].astype(jnp.bfloat16)
        return 0

    lax.fori_loop(0, bands, finish, 0)


def tile_kernel(got, out, wide):
    peers = got.shape[0] // PEER_ROWS
    part = 4 * PEER_ROWS

    def widen(p, _):
        piece = pl.ds(pl.multiple_of(p * part, 16), part)
        wide[piece, :] = got[piece, :].astype(jnp.float32)
        return 0

    lax.fori_loop(0, peers // 4, widen, 0)

    def line_of_all(row):
        return wide[pl.ds(row, peers, stride=PEER_ROWS), :]

    lanes = lax.broadcasted_iota(jnp.int32, (peers, 128), 1)
    row_id = lanes.astype(jnp.float32)
    place = lanes % EDGE
    shared = line_of_all(OWN_ROWS + CAP)
    stencil, spill_next, spill_prev = [], [], []
    for j in range(CAP):
        line = line_of_all(OWN_ROWS + j)
        table = jnp.zeros((peers, 128), jnp.float32)
        start = line[:, META : META + 1]
        for k in range(4):
            table = table + jnp.where(row_id == start + float(k), line[:, META + 2 + k : META + 3 + k], 0.0)
        stencil.append(table.T.astype(jnp.bfloat16))
        shift = line[:, META + 1 : META + 2]
        forward = (shift > 0.5) | ((shift > -1.5) & (place < EDGE // 2))
        rest = pltpu.roll(shared, (128 - 4 * EDGE * j) % 128, 1) if j else shared
        both = [line, rest]
        spill_next.append(jnp.concatenate([jnp.where(forward, s, 0.0) for s in both], axis=1).astype(jnp.bfloat16))
        spill_prev.append(jnp.concatenate([jnp.where(forward, 0.0, s) for s in both], axis=1).astype(jnp.bfloat16))
    columns = jnp.concatenate(stencil, axis=1)

    def product(values):
        return jnp.dot(columns, jnp.concatenate(values, axis=0), preferred_element_type=jnp.float32)

    onward = product(spill_next)
    onward = jnp.concatenate([onward[128 - TL :], onward[: 128 - TL]], axis=0)
    back = product(spill_prev)
    back = jnp.concatenate([back[TL:], back[:TL]], axis=0)
    lane = lax.broadcasted_iota(jnp.int32, (128, 128), 1)
    for pair in range(8):
        values = []
        for j in range(CAP):
            cols = [line_of_all(j * SLOT_ROWS + 2 * pair + e).astype(jnp.bfloat16) for e in range(2)]
            values.append(jnp.concatenate(cols, axis=1))
        total = product(values)
        for e in range(2):
            fl = 2 * pair + e
            h, i = fl // WHOLE, fl % WHOLE
            ahead = pltpu.roll(onward[:, 128 * h : 128 * h + 128], (128 - EDGE * i) % 128, 1)
            behind = pltpu.roll(back[:, 128 * h : 128 * h + 128], (256 - EDGE - EDGE * i) % 128, 1)
            around = jnp.where(lane < EDGE, ahead, jnp.where(lane >= 128 - EDGE, behind, 0.0))
            out[fl % 4, fl // 4] = total[:, 128 * e : 128 * e + 128] + around


def local(increments, band, tile_index, lat_offset, lon_shift, lat_frac, lon_frac):
    rows = increments.shape[0]
    n_lat = lax.axis_size("lat")
    peers = 4 * n_lat
    hbm = pl.BlockSpec(memory_space=pltpu.HBM)
    vmem = pl.BlockSpec(memory_space=pltpu.VMEM)
    whole = (peers * PEER_ROWS, 128)
    send = pl.pallas_call(
        source_kernel,
        out_shape=jax.ShapeDtypeStruct(whole, jnp.bfloat16),
        in_specs=[hbm] * 7,
        out_specs=vmem,
        scratch_shapes=[pltpu.SMEM((rows,), jnp.int32)] * 4
        + [pltpu.SMEM((rows,), jnp.float32), pltpu.SMEM((n_lat,), jnp.int32)]
        + [pltpu.SMEM((rows,), jnp.int32)] * 2
        + [
            pltpu.VMEM(increments.shape, jnp.bfloat16),
            pltpu.VMEM((rows, 128), jnp.float32),
            pltpu.VMEM((4, rows, 128), jnp.float32),
            pltpu.VMEM(whole, jnp.float32),
            pltpu.VMEM((rows * 64, 128), jnp.float32),
            pltpu.VMEM((rows, 128), jnp.float32),
            pltpu.VMEM((8, rows, 128), jnp.float32),
            pltpu.SemaphoreType.DMA((7,)),
        ],
        compiler_params=pltpu.CompilerParams(vmem_limit_bytes=60 << 20),
        name="lon_slots",
    )(band.reshape(rows), tile_index, lat_offset, lon_shift, lat_frac, increments, lon_frac)
    fine = (peers * PEER_ROWS // 4, 4, 128)
    got = lax.all_to_all(send.reshape(fine), ("lat", "grp"), 0, 0, tiled=True)
    return pl.pallas_call(
        tile_kernel,
        out_shape=jax.ShapeDtypeStruct((4, 4, 128, 128), jnp.float32),
        in_specs=[vmem],
        out_specs=vmem,
        scratch_shapes=[pltpu.VMEM(whole, jnp.float32)],
        compiler_params=pltpu.CompilerParams(vmem_limit_bytes=40 << 20),
        name="tile_sums",
    )(got.reshape(whole))


def solution(mesh):
    in_specs = (
        P(("lat", "grp"), None, None, None),
        P(("lat", "grp"), None),
        P(("lat", "grp")),
        P(("lat", "grp")),
        P(("lat", "grp")),
        P(("lat", "grp")),
        P(("lat", "grp"), None),
    )
    out_specs = P("grp", None, "lat", None)
    return jax.shard_map(local, mesh=mesh, in_specs=in_specs, out_specs=out_specs, check_vma=False)
```

```python
import jax
import jax.numpy as jnp
from jax import lax
from jax.experimental import pallas as pl
from jax.experimental.pallas import tpu as pltpu
from jax.sharding import PartitionSpec as P

TL = 16
CAP = 3
SLOT_ROWS = 16
OWN_ROWS = CAP * SLOT_ROWS
PEER_ROWS = OWN_ROWS + CAP + 1
EDGE = 10
WHOLE = 12
META = EDGE * WHOLE
PITCH = 65
OUT_PARTS = 8


def lagrange(fraction):
    return [
        -fraction * (fraction - 1.0) * (fraction - 2.0) / 6.0,
        (fraction + 1.0) * (fraction - 1.0) * (fraction - 2.0) / 2.0,
        -(fraction + 1.0) * fraction * (fraction - 2.0) / 2.0,
        (fraction + 1.0) * fraction * (fraction - 1.0) / 6.0,
    ]


def rounded(x):
    return x.astype(jnp.bfloat16).astype(jnp.float32)


def source_kernel(
    band_hbm, tile_hbm, offset_hbm, shift_hbm, lat_hbm, inc_hbm, lon_hbm, out,
    band, tile_index, lat_offset, lon_shift, lat_frac, count, first, slot_of,
    inc, lon_frac, weights, stage, packed, edges, meta_lines, lines, rests, sems, out_sems,
):
    rows = inc.shape[0]
    bands = count.shape[0]
    pairs = (
        (band_hbm, band), (tile_hbm, tile_index), (offset_hbm, lat_offset), (shift_hbm, lon_shift),
        (lat_hbm, lat_frac), (lon_hbm, lon_frac), (inc_hbm, inc),
    )
    copies = [pltpu.make_async_copy(src, dst, sems.at[i]) for i, (src, dst) in enumerate(pairs)]
    for copy in copies:
        copy.start()

    lane = lax.broadcasted_iota(jnp.int32, (8, 128), 1)
    sub = lax.broadcasted_iota(jnp.int32, (8, 128), 0)
    zero = jnp.zeros((8, 128), jnp.float32)
    part = stage.shape[0] // bands

    def clear(i, _):
        stage[pl.ds(pl.multiple_of(i * part, 8), part), :] = jnp.zeros((part, 128), jnp.float32)
        count[i] = 0
        return 0

    lax.fori_loop(0, bands, clear, 0)
    for copy in copies:
        copy.wait()

    for m, w in enumerate(lagrange(lon_frac[...])):
        weights[m] = rounded(w)

    def one_row(r, _):
        b = band[r]
        slot = count[b]
        count[b] = slot + 1
        slot_of[r] = slot
        peer_row = b * (4 * PEER_ROWS)
        first[r] = peer_row
        shift = lon_shift[r]
        x = inc[r].astype(jnp.float32)
        half = [[x[f, 8 * h : 8 * h + 8] for h in range(2)] for f in range(4)]
        pieces = []
        for g in range(4):
            h, odd = g // 2, g % 2
            for f in (0, 2):
                upper, lower = half[f][h], half[f + 1][h]
                if odd:
                    upper = pltpu.roll(upper, 4, 0)
                else:
                    lower = pltpu.roll(lower, 4, 0)
                pieces.append(jnp.where(sub < 4, upper, lower))
        own = [None] * 8
        spill = [None] * 8
        for m in range(4):
            move = (shift + (m - 1 + 128)) & 127
            w = jnp.broadcast_to(weights[m, pl.ds(r, 1), :], (8, 128))
            w = pltpu.roll(w, move, 1)
            raw = lane - shift - (m - 1)
            inside = (raw >= 0) & (raw < 128)
            own_w = jnp.where(inside, w, 0.0)
            spill_w = jnp.where(inside, 0.0, w)
            for i in range(8):
                moved = pltpu.roll(pieces[i], move, 1)
                own[i] = own_w * moved if m == 0 else own[i] + own_w * moved
                spill[i] = spill_w * moved if m == 0 else spill[i] + spill_w * moved
        for i in range(8):
            stage[pl.ds(peer_row + (i // 2) * PEER_ROWS + slot * SLOT_ROWS + 8 * (i % 2), 8), :] = own[i]
            edges[pl.ds(r * PITCH + 8 * i, 8), :] = spill[i]
        start = (tile_index[r] * TL + lat_offset[r]).astype(jnp.float32)
        meta = jnp.where(lane == META, start, jnp.where(lane == META + 1, shift.astype(jnp.float32), 0.0))
        meta = jnp.where(lane > META + 1, lat_frac[r], meta)
        meta_lines[pl.ds(r, 1), :] = meta[0:1]
        return 0

    lax.fori_loop(0, rows, one_row, 0, unroll=4)

    def pack(n, _):
        rows_here = pl.ds(pl.multiple_of(8 * n, 8), 8)
        meta = meta_lines[rows_here, :]
        for k, w in enumerate(lagrange(meta)):
            meta = jnp.where(lane == META + 2 + k, w, meta)
        meta = jnp.where(lane < META + 6, meta, 0.0)
        for g in range(4):
            whole = meta
            rest = None
            for fl in range(SLOT_ROWS):
                line = edges[pl.ds(n * (8 * PITCH) + g * SLOT_ROWS + fl, 8, stride=PITCH), :]
                line = jnp.where(lane < EDGE, line + pltpu.roll(line, EDGE, 1), 0.0)
                if fl < WHOLE:
                    whole = whole + (pltpu.roll(line, EDGE * fl, 1) if fl else line)
                else:
                    line = pltpu.roll(line, EDGE * (fl - WHOLE), 1) if fl > WHOLE else line
                    rest = line if rest is None else rest + line
            lines[g, rows_here, :] = whole
            for slot in range(CAP):
                lines[4 + CAP * g + slot, rows_here, :] = pltpu.roll(rest, 4 * EDGE * slot, 1) if slot else rest
        return 0

    lax.fori_loop(0, rows // 8, pack, 0)
    rests[...] = jnp.zeros(rests.shape, jnp.float32)

    def place(r, _):
        slot = slot_of[r]
        row = pl.ds(r, 1)
        at = first[r] + OWN_ROWS + slot
        peer = band[r] * 4
        for g in range(4):
            stage[pl.ds(at + g * PEER_ROWS, 1), :] = lines[g, row, :]
            rests[slot, pl.ds(peer + g, 1), :] = lines[4 + CAP * g + slot, row, :]
        return 0

    lax.fori_loop(0, rows, place, 0, unroll=8)
    stage[pl.ds(OWN_ROWS + CAP, 4 * bands, stride=PEER_ROWS), :] = rests[0] + rests[1] + rests[2]

    size = stage.shape[0] // OUT_PARTS
    sends = []
    for n in range(OUT_PARTS):

        def finish(i, _):
            piece = pl.ds(pl.multiple_of(n * size + i * part, 16), part)
            packed[piece, :] = stage[piece, :].astype(jnp.bfloat16)
            return 0

        lax.fori_loop(0, bands // OUT_PARTS, finish, 0)
        span = pl.ds(n * size, size)
        sends.append(pltpu.make_async_copy(packed.at[span, :], out.at[span, :], out_sems.at[n]))
        sends[-1].start()
    for send in sends:
        send.wait()


def tile_kernel(got, out, wide):
    peers = got.shape[0] // PEER_ROWS
    part = 4 * PEER_ROWS

    def widen(p, _):
        piece = pl.ds(pl.multiple_of(p * part, 16), part)
        wide[piece, :] = got[piece, :].astype(jnp.float32)
        return 0

    lax.fori_loop(0, peers // 4, widen, 0)

    def line_of_all(row):
        return wide[pl.ds(row, peers, stride=PEER_ROWS), :]

    lanes = lax.broadcasted_iota(jnp.int32, (peers, 128), 1)
    row_id = lanes.astype(jnp.float32)
    place = lanes % EDGE
    shared = line_of_all(OWN_ROWS + CAP)
    stencil, spill_next, spill_prev = [], [], []
    for j in range(CAP):
        line = line_of_all(OWN_ROWS + j)
        table = jnp.zeros((peers, 128), jnp.float32)
        start = line[:, META : META + 1]
        for k in range(4):
            table = table + jnp.where(row_id == start + float(k), line[:, META + 2 + k : META + 3 + k], 0.0)
        stencil.append(table.T.astype(jnp.bfloat16))
        shift = line[:, META + 1 : META + 2]
        forward = (shift > 0.5) | ((shift > -1.5) & (place < EDGE // 2))
        rest = pltpu.roll(shared, (128 - 4 * EDGE * j) % 128, 1) if j else shared
        both = [line, rest]
        spill_next.append(jnp.concatenate([jnp.where(forward, s, 0.0) for s in both], axis=1).astype(jnp.bfloat16))
        spill_prev.append(jnp.concatenate([jnp.where(forward, 0.0, s) for s in both], axis=1).astype(jnp.bfloat16))
    columns = jnp.concatenate(stencil, axis=1)

    def product(values):
        return jnp.dot(columns, jnp.concatenate(values, axis=0), preferred_element_type=jnp.float32)

    onward = product(spill_next)
    onward = jnp.concatenate([onward[128 - TL :], onward[: 128 - TL]], axis=0)
    back = product(spill_prev)
    back = jnp.concatenate([back[TL:], back[:TL]], axis=0)
    lane = lax.broadcasted_iota(jnp.int32, (128, 128), 1)
    for pair in range(8):
        values = []
        for j in range(CAP):
            cols = [line_of_all(j * SLOT_ROWS + 2 * pair + e).astype(jnp.bfloat16) for e in range(2)]
            values.append(jnp.concatenate(cols, axis=1))
        total = product(values)
        for e in range(2):
            fl = 2 * pair + e
            h, i = fl // WHOLE, fl % WHOLE
            ahead = pltpu.roll(onward[:, 128 * h : 128 * h + 128], (128 - EDGE * i) % 128, 1)
            behind = pltpu.roll(back[:, 128 * h : 128 * h + 128], (256 - EDGE - EDGE * i) % 128, 1)
            around = jnp.where(lane < EDGE, ahead, jnp.where(lane >= 128 - EDGE, behind, 0.0))
            out[fl % 4, fl // 4] = total[:, 128 * e : 128 * e + 128] + around


def local(increments, band, tile_index, lat_offset, lon_shift, lat_frac, lon_frac):
    rows = increments.shape[0]
    n_lat = lax.axis_size("lat")
    peers = 4 * n_lat
    hbm = pl.BlockSpec(memory_space=pltpu.HBM)
    vmem = pl.BlockSpec(memory_space=pltpu.VMEM)
    whole = (peers * PEER_ROWS, 128)
    send = pl.pallas_call(
        source_kernel,
        out_shape=jax.ShapeDtypeStruct(whole, jnp.bfloat16),
        in_specs=[hbm] * 7,
        out_specs=hbm,
        scratch_shapes=[pltpu.SMEM((rows,), jnp.int32)] * 4
        + [pltpu.SMEM((rows,), jnp.float32), pltpu.SMEM((n_lat,), jnp.int32)]
        + [pltpu.SMEM((rows,), jnp.int32)] * 2
        + [
            pltpu.VMEM(increments.shape, jnp.bfloat16),
            pltpu.VMEM((rows, 128), jnp.float32),
            pltpu.VMEM((4, rows, 128), jnp.float32),
            pltpu.VMEM(whole, jnp.float32),
            pltpu.VMEM(whole, jnp.bfloat16),
            pltpu.VMEM((rows * PITCH, 128), jnp.float32),
            pltpu.VMEM((rows, 128), jnp.float32),
            pltpu.VMEM((4 + 4 * CAP, rows, 128), jnp.float32),
            pltpu.VMEM((CAP, peers, 128), jnp.float32),
            pltpu.SemaphoreType.DMA((7,)),
            pltpu.SemaphoreType.DMA((OUT_PARTS,)),
        ],
        compiler_params=pltpu.CompilerParams(vmem_limit_bytes=60 << 20),
        name="lon_slots",
    )(band.reshape(rows), tile_index, lat_offset, lon_shift, lat_frac, increments, lon_frac)
    fine = (peers * PEER_ROWS // 4, 4, 128)
    got = lax.all_to_all(send.reshape(fine), ("lat", "grp"), 0, 0, tiled=True)
    return pl.pallas_call(
        tile_kernel,
        out_shape=jax.ShapeDtypeStruct((4, 4, 128, 128), jnp.float32),
        in_specs=[vmem],
        out_specs=vmem,
        scratch_shapes=[pltpu.VMEM(whole, jnp.float32)],
        compiler_params=pltpu.CompilerParams(vmem_limit_bytes=40 << 20),
        name="tile_sums",
    )(got.reshape(whole))


def solution(mesh):
    in_specs = (
        P(("lat", "grp"), None, None, None),
        P(("lat", "grp"), None),
        P(("lat", "grp")),
        P(("lat", "grp")),
        P(("lat", "grp")),
        P(("lat", "grp")),
        P(("lat", "grp"), None),
    )
    out_specs = P("grp", None, "lat", None)
    return jax.shard_map(local, mesh=mesh, in_specs=in_specs, out_specs=out_specs, check_vma=False)
```

```python
import jax
import jax.numpy as jnp
from jax import lax
from jax.experimental import pallas as pl
from jax.experimental.pallas import tpu as pltpu
from jax.sharding import PartitionSpec as P

TL = 16
CAP = 3
SLOT_ROWS = 16
OWN_ROWS = CAP * SLOT_ROWS
PEER_ROWS = OWN_ROWS + 2
OVER = 3
META = OVER * SLOT_ROWS
FIELD = 16
PITCH = 65
OUT_PARTS = 8
SPARE = 72


def lagrange(fraction):
    return [
        -fraction * (fraction - 1.0) * (fraction - 2.0) / 6.0,
        (fraction + 1.0) * (fraction - 1.0) * (fraction - 2.0) / 2.0,
        -(fraction + 1.0) * fraction * (fraction - 2.0) / 2.0,
        (fraction + 1.0) * fraction * (fraction - 1.0) / 6.0,
    ]


def rounded(x):
    return x.astype(jnp.bfloat16).astype(jnp.float32)


def source_kernel(
    band_hbm, tile_hbm, offset_hbm, shift_hbm, lat_hbm, inc_hbm, lon_hbm, out,
    band, tile_index, lat_offset, lon_shift, lat_frac, count, slot_of,
    inc, lon_frac, weights, stage, packed, edges, meta_lines, lines, rests, sems, out_sems,
):
    rows = inc.shape[0]
    bands = count.shape[0]
    pairs = (
        (band_hbm, band), (tile_hbm, tile_index), (offset_hbm, lat_offset), (shift_hbm, lon_shift),
        (lat_hbm, lat_frac), (lon_hbm, lon_frac), (inc_hbm, inc),
    )
    copies = [pltpu.make_async_copy(src, dst, sems.at[i]) for i, (src, dst) in enumerate(pairs)]
    for copy in copies:
        copy.start()

    lane = lax.broadcasted_iota(jnp.int32, (8, 128), 1)
    sub = lax.broadcasted_iota(jnp.int32, (8, 128), 0)
    zero = jnp.zeros((8, 128), jnp.float32)
    part = out.shape[0] // (bands // 2)

    def clear(i, _):
        stage[pl.ds(pl.multiple_of(i * part, 8), part), :] = jnp.zeros((part, 128), jnp.float32)
        count[2 * i] = 0
        count[2 * i + 1] = 0
        return 0

    lax.fori_loop(0, bands // 2, clear, 0)
    rests[...] = jnp.zeros(rests.shape, jnp.float32)
    for copy in copies:
        copy.wait()

    for m, w in enumerate(lagrange(lon_frac[...])):
        weights[m] = rounded(w)

    def one_row(r, _):
        b = band[r]
        slot = count[b]
        count[b] = slot + 1
        slot_of[r] = slot
        peer_row = b * (4 * PEER_ROWS)
        shift = lon_shift[r]
        x = inc[r].astype(jnp.float32)
        pieces = [x[i // 2, 8 * (i % 2) : 8 * (i % 2) + 8] for i in range(8)]
        own = [None] * 8
        over = [None] * 8
        for m in range(4):
            move = (shift + (m - 1 + 128)) & 127
            w = jnp.broadcast_to(weights[m, pl.ds(r, 1), :], (8, 128))
            w = pltpu.roll(w, move, 1)
            inside = ((lane - shift - (m - 1)) & 127) < 128 - m
            own_w = jnp.where(inside, w, 0.0)
            over_w = jnp.where(inside, 0.0, w)
            for i in range(8):
                moved = pltpu.roll(pieces[i], move, 1)
                own[i] = own_w * moved if m == 0 else own[i] + own_w * moved
                if m > 0:
                    over[i] = over_w * moved if m == 1 else over[i] + over_w * moved
        at = peer_row + slot * SLOT_ROWS
        for i in range(8):
            f, h = i // 2, i % 2
            low = pl.ds(at + 2 * h * PEER_ROWS + 4 * f, 8)
            pltpu.store(stage.at[low, :], own[i], mask=sub < 4)
            high = pl.ds(at + (2 * h + 1) * PEER_ROWS + 4 * f - 4, 8)
            pltpu.store(stage.at[high, :], own[i], mask=sub >= 4)
            edges[pl.ds(r * PITCH + 8 * i, 8), :] = over[i]
        start = (tile_index[r] * TL + lat_offset[r]).astype(jnp.float32)
        meta = jnp.where(lane == META, start, jnp.where(lane == META + 1, shift.astype(jnp.float32), 0.0))
        meta = jnp.where(lane > META + 1, lat_frac[r], meta)
        meta_lines[pl.ds(r, 1), :] = meta[0:1]
        return 0

    lax.fori_loop(0, rows, one_row, 0, unroll=8)

    def align(r, _):
        back = (129 - lon_shift[r]) & 127
        for i in range(8):
            piece = pl.ds(r * PITCH + 8 * i, 8)
            edges[piece, :] = pltpu.roll(edges[piece, :], back, 1)
        return 0

    lax.fori_loop(0, rows, align, 0, unroll=8)

    def pack(n, _):
        rows_here = pl.ds(pl.multiple_of(8 * n, 8), 8)
        meta = meta_lines[rows_here, :]
        for k, w in enumerate(lagrange(meta)):
            meta = jnp.where(lane == META + 2 + k, w, meta)
        meta = jnp.where((lane >= META) & (lane < META + 6), meta, 0.0)
        for g in range(4):
            whole = meta
            for fl in range(SLOT_ROWS):
                line = edges[pl.ds(n * (8 * PITCH) + (fl // 4) * 16 + 4 * g + fl % 4, 8, stride=PITCH), :]
                whole = whole + (pltpu.roll(line, OVER * fl, 1) if fl else line)
            lines[g, rows_here, :] = whole
            lines[4 + g, rows_here, :] = pltpu.roll(whole, 64, 1)
        return 0

    lax.fori_loop(0, rows // 8, pack, 0)

    def place(r, _):
        slot = slot_of[r]
        row = pl.ds(r, 1)
        peer = band[r] * 4
        side = jnp.where(slot == 1, 4, 0)
        for g in range(4):
            rests[slot, pl.ds(peer + g, 1), :] = lines[side + g, row, :]
        return 0

    lax.fori_loop(0, rows, place, 0, unroll=8)
    stage[pl.ds(OWN_ROWS, 4 * bands, stride=PEER_ROWS), :] = rests[0] + rests[1]
    stage[pl.ds(OWN_ROWS + 1, 4 * bands, stride=PEER_ROWS), :] = rests[2]

    size = out.shape[0] // OUT_PARTS
    sends = []
    for n in range(OUT_PARTS):

        def finish(i, _):
            piece = pl.ds(pl.multiple_of(n * size + i * part, 16), part)
            packed[piece, :] = stage[piece, :].astype(jnp.bfloat16)
            return 0

        lax.fori_loop(0, bands // (2 * OUT_PARTS), finish, 0)
        span = pl.ds(n * size, size)
        sends.append(pltpu.make_async_copy(packed.at[span, :], out.at[span, :], out_sems.at[n]))
        sends[-1].start()
    for send in sends:
        send.wait()


def tile_kernel(got, out, wide, result, sems):
    peers = got.shape[0] // PEER_ROWS
    part = 8 * PEER_ROWS

    def widen(p, _):
        piece = pl.ds(pl.multiple_of(p * part, 16), part)
        wide[piece, :] = got[piece, :].astype(jnp.float32)
        return 0

    lax.fori_loop(0, peers // 8, widen, 0)

    def line_of_all(row):
        return wide[pl.ds(row, peers, stride=PEER_ROWS), :]

    lanes = lax.broadcasted_iota(jnp.int32, (peers, 128), 1)
    row_id = lanes.astype(jnp.float32)
    field, place = lanes // FIELD, lanes % FIELD
    pair_line = line_of_all(OWN_ROWS)
    slot_lines = [pair_line, pltpu.roll(pair_line, 64, 1), line_of_all(OWN_ROWS + 1)]
    stencil, here, over_next, over_own = [], [], [], []
    for line in slot_lines:
        table = jnp.zeros((peers, 128), jnp.float32)
        start = line[:, META : META + 1]
        for k in range(4):
            table = table + jnp.where(row_id == start + float(k), line[:, META + 2 + k : META + 3 + k], 0.0)
        stencil.append(table.T.astype(jnp.bfloat16))
        shift = jnp.broadcast_to(line[:, META + 1 : META + 2], (peers, 128)).astype(jnp.int32)
        step = lanes - shift
        mask = jnp.where((step >= -1) & (step <= 126), 1.0, 0.0).astype(jnp.bfloat16)
        here.append(jnp.concatenate([mask, mask], axis=1))
        ahead = place - shift + 1
        local_e = ahead - FIELD
        is_next = (ahead >= 0) & (ahead <= 2)
        is_own = (local_e >= 0) & (local_e <= 2)
        column = jnp.where(is_own, local_e, jnp.where(is_next, ahead, 0))
        nexts, owns = [], []
        for h in range(2):
            picked = jnp.take_along_axis(line, column + OVER * (field + 8 * h), axis=1)
            nexts.append(jnp.where(is_next, picked, 0.0))
            owns.append(jnp.where(is_own, picked, 0.0))
        over_next.append(jnp.concatenate(nexts, axis=1).astype(jnp.bfloat16))
        over_own.append(jnp.concatenate(owns, axis=1).astype(jnp.bfloat16))
    columns = jnp.concatenate(stencil, axis=1)
    here = jnp.concatenate(here, axis=0)

    def product(values):
        return jnp.dot(columns, values, preferred_element_type=jnp.float32)

    def later(x):
        return jnp.concatenate([x[128 - TL :], x[: 128 - TL]], axis=0)

    def earlier(x):
        return jnp.concatenate([x[TL:], x[:TL]], axis=0)

    onward = later(product(jnp.concatenate(over_next, axis=0)))
    local_over = product(jnp.concatenate(over_own, axis=0))
    lane = lax.broadcasted_iota(jnp.int32, (128, 128), 1)
    sends = []
    for pair in range(8):
        values = []
        for j in range(CAP):
            cols = [line_of_all(j * SLOT_ROWS + 2 * pair + e).astype(jnp.bfloat16) for e in range(2)]
            values.append(jnp.concatenate(cols, axis=1))
        values = jnp.concatenate(values, axis=0)
        staying = values * here
        total = product(staying)
        moving = product(values - staying)
        for e in range(2):
            fl = 2 * pair + e
            h, i = fl // 8, fl % 8
            ahead = pltpu.roll(onward[:, 128 * h : 128 * h + 128], (128 - FIELD * i) % 128, 1)
            behind = pltpu.roll(local_over[:, 128 * h : 128 * h + 128], (256 - FIELD - FIELD * i) % 128, 1)
            around = jnp.where(lane < FIELD, ahead, jnp.where(lane >= 128 - FIELD, behind, 0.0))
            part_moving = moving[:, 128 * e : 128 * e + 128]
            around = around + jnp.where(lane < 64, later(part_moving), earlier(part_moving))
            spot = (fl % 4, fl // 4)
            result[spot] = total[:, 128 * e : 128 * e + 128] + around
            sends.append(pltpu.make_async_copy(result.at[spot], out.at[spot], sems.at[fl]))
            sends[-1].start()
    for send in sends:
        send.wait()


def local(increments, band, tile_index, lat_offset, lon_shift, lat_frac, lon_frac):
    rows = increments.shape[0]
    n_lat = lax.axis_size("lat")
    peers = 4 * n_lat
    hbm = pl.BlockSpec(memory_space=pltpu.HBM)
    vmem = pl.BlockSpec(memory_space=pltpu.VMEM)
    whole = (peers * PEER_ROWS, 128)
    roomy = (peers * PEER_ROWS + SPARE, 128)
    send = pl.pallas_call(
        source_kernel,
        out_shape=jax.ShapeDtypeStruct(whole, jnp.bfloat16),
        in_specs=[hbm] * 7,
        out_specs=hbm,
        scratch_shapes=[pltpu.SMEM((rows,), jnp.int32)] * 4
        + [pltpu.SMEM((rows,), jnp.float32), pltpu.SMEM((n_lat,), jnp.int32)]
        + [pltpu.SMEM((rows,), jnp.int32)]
        + [
            pltpu.VMEM(increments.shape, jnp.bfloat16),
            pltpu.VMEM((rows, 128), jnp.float32),
            pltpu.VMEM((4, rows, 128), jnp.float32),
            pltpu.VMEM(roomy, jnp.float32),
            pltpu.VMEM(whole, jnp.bfloat16),
            pltpu.VMEM((rows * PITCH + SPARE, 128), jnp.float32),
            pltpu.VMEM((rows, 128), jnp.float32),
            pltpu.VMEM((8, rows, 128), jnp.float32),
            pltpu.VMEM((CAP, peers, 128), jnp.float32),
            pltpu.SemaphoreType.DMA((7,)),
            pltpu.SemaphoreType.DMA((OUT_PARTS,)),
        ],
        compiler_params=pltpu.CompilerParams(vmem_limit_bytes=60 << 20),
        name="lon_slots",
    )(band.reshape(rows), tile_index, lat_offset, lon_shift, lat_frac, increments, lon_frac)
    fine = (peers * PEER_ROWS // 2, 2, 128)
    got = lax.all_to_all(send.reshape(fine), ("lat", "grp"), 0, 0, tiled=True)
    return pl.pallas_call(
        tile_kernel,
        out_shape=jax.ShapeDtypeStruct((4, 4, 128, 128), jnp.float32),
        in_specs=[vmem],
        out_specs=hbm,
        scratch_shapes=[
            pltpu.VMEM(roomy, jnp.float32),
            pltpu.VMEM((4, 4, 128, 128), jnp.float32),
            pltpu.SemaphoreType.DMA((SLOT_ROWS,)),
        ],
        compiler_params=pltpu.CompilerParams(vmem_limit_bytes=40 << 20),
        name="tile_sums",
    )(got.reshape(whole))


def solution(mesh):
    in_specs = (
        P(("lat", "grp"), None, None, None),
        P(("lat", "grp"), None),
        P(("lat", "grp")),
        P(("lat", "grp")),
        P(("lat", "grp")),
        P(("lat", "grp")),
        P(("lat", "grp"), None),
    )
    out_specs = P("grp", None, "lat", None)
    return jax.shard_map(local, mesh=mesh, in_specs=in_specs, out_specs=out_specs, check_vma=False)
```

```python
import jax
import jax.numpy as jnp
from jax import lax
from jax.experimental import pallas as pl
from jax.experimental.pallas import tpu as pltpu
from jax.sharding import PartitionSpec as P

TL = 16
CAP = 3
SLOT_ROWS = 16
OWN_ROWS = CAP * SLOT_ROWS
PEER_ROWS = OWN_ROWS + 2
OVER = 3
META = OVER * SLOT_ROWS
FIELD = 16
PITCH = 65
OUT_PARTS = 8
SPARE = 72


def lagrange(fraction):
    return [
        -fraction * (fraction - 1.0) * (fraction - 2.0) / 6.0,
        (fraction + 1.0) * (fraction - 1.0) * (fraction - 2.0) / 2.0,
        -(fraction + 1.0) * fraction * (fraction - 2.0) / 2.0,
        (fraction + 1.0) * fraction * (fraction - 1.0) / 6.0,
    ]


def rounded(x):
    return x.astype(jnp.bfloat16).astype(jnp.float32)


def source_kernel(
    band_hbm, tile_hbm, offset_hbm, shift_hbm, lat_hbm, inc_hbm, lon_hbm, out,
    band, tile_index, lat_offset, lon_shift, lat_frac, count, slot_of,
    inc, lon_frac, weights, stage, packed, edges, meta_lines, lines, rests, sems, out_sems,
):
    rows = inc.shape[0]
    bands = count.shape[0]
    pairs = (
        (band_hbm, band), (tile_hbm, tile_index), (offset_hbm, lat_offset), (shift_hbm, lon_shift),
        (lat_hbm, lat_frac),
    )
    pairs = ((inc_hbm, inc), (lon_hbm, lon_frac)) + pairs
    copies = [pltpu.make_async_copy(src, dst, sems.at[i]) for i, (src, dst) in enumerate(pairs)]
    for copy in copies:
        copy.start()

    lane = lax.broadcasted_iota(jnp.int32, (8, 128), 1)
    sub = lax.broadcasted_iota(jnp.int32, (8, 128), 0)
    zero = jnp.zeros((8, 128), jnp.float32)
    part = out.shape[0] // (bands // 2)

    def clear(i, _):
        stage[pl.ds(pl.multiple_of(i * part, 8), part), :] = jnp.zeros((part, 128), jnp.float32)
        count[2 * i] = 0
        count[2 * i + 1] = 0
        return 0

    lax.fori_loop(0, bands // 2, clear, 0)
    rests[...] = jnp.zeros(rests.shape, jnp.float32)
    copies[1].wait()

    for m, w in enumerate(lagrange(lon_frac[...])):
        weights[m] = rounded(w)

    for copy in copies[2:]:
        copy.wait()
    copies[0].wait()

    def one_row(r, _):
        b = band[r]
        slot = count[b]
        count[b] = slot + 1
        slot_of[r] = slot
        peer_row = b * (4 * PEER_ROWS)
        shift = lon_shift[r]
        x = inc[r].astype(jnp.float32)
        pieces = [x[i // 2, 8 * (i % 2) : 8 * (i % 2) + 8] for i in range(8)]
        own = [None] * 8
        over = [None] * 8
        for m in range(4):
            move = (shift + (m - 1 + 128)) & 127
            w = jnp.broadcast_to(weights[m, pl.ds(r, 1), :], (8, 128))
            w = pltpu.roll(w, move, 1)
            inside = ((lane - shift - (m - 1)) & 127) < 128 - m
            own_w = jnp.where(inside, w, 0.0)
            over_w = jnp.where(inside, 0.0, w)
            for i in range(8):
                moved = pltpu.roll(pieces[i], move, 1)
                own[i] = own_w * moved if m == 0 else own[i] + own_w * moved
                if m > 0:
                    over[i] = over_w * moved if m == 1 else over[i] + over_w * moved
        at = peer_row + slot * SLOT_ROWS
        for i in range(8):
            f, h = i // 2, i % 2
            low = pl.ds(at + 2 * h * PEER_ROWS + 4 * f, 8)
            pltpu.store(stage.at[low, :], own[i], mask=sub < 4)
            high = pl.ds(at + (2 * h + 1) * PEER_ROWS + 4 * f - 4, 8)
            pltpu.store(stage.at[high, :], own[i], mask=sub >= 4)
            edges[pl.ds(r * PITCH + 8 * i, 8), :] = over[i]
        start = (tile_index[r] * TL + lat_offset[r]).astype(jnp.float32)
        meta = jnp.where(lane == META, start, jnp.where(lane == META + 1, shift.astype(jnp.float32), 0.0))
        meta = jnp.where(lane > META + 1, lat_frac[r], meta)
        meta_lines[pl.ds(r, 1), :] = meta[0:1]
        return 0

    lax.fori_loop(0, rows, one_row, 0, unroll=16)

    def pack(n, _):
        rows_here = pl.ds(pl.multiple_of(8 * n, 8), 8)
        meta = meta_lines[rows_here, :]
        shift = jnp.broadcast_to(meta[:, META + 1 : META + 2], (8, 128)).astype(jnp.int32)
        origin = (shift + 127 + lane % OVER) & 127
        for k, w in enumerate(lagrange(meta)):
            meta = jnp.where(lane == META + 2 + k, w, meta)
        meta = jnp.where((lane >= META) & (lane < META + 6), meta, 0.0)
        for g in range(4):
            whole = meta
            for fl in range(SLOT_ROWS):
                line = edges[pl.ds(n * (8 * PITCH) + (fl // 4) * 16 + 4 * g + fl % 4, 8, stride=PITCH), :]
                whole = jnp.where(lane // OVER == fl, jnp.take_along_axis(line, origin, axis=1), whole)
            lines[g, rows_here, :] = whole
            lines[4 + g, rows_here, :] = pltpu.roll(whole, 64, 1)
        return 0

    lax.fori_loop(0, rows // 8, pack, 0, unroll=2)

    def place(r, _):
        slot = slot_of[r]
        row = pl.ds(r, 1)
        peer = band[r] * 4
        side = jnp.where(slot == 1, 4, 0)
        for g in range(4):
            rests[slot, pl.ds(peer + g, 1), :] = lines[side + g, row, :]
        return 0

    lax.fori_loop(0, rows, place, 0, unroll=8)
    stage[pl.ds(OWN_ROWS, 4 * bands, stride=PEER_ROWS), :] = rests[0] + rests[1]
    stage[pl.ds(OWN_ROWS + 1, 4 * bands, stride=PEER_ROWS), :] = rests[2]

    size = out.shape[0] // OUT_PARTS
    sends = []
    for n in range(OUT_PARTS):

        def finish(i, _):
            piece = pl.ds(pl.multiple_of(n * size + i * part, 16), part)
            packed[piece, :] = stage[piece, :].astype(jnp.bfloat16)
            return 0

        lax.fori_loop(0, bands // (2 * OUT_PARTS), finish, 0)
        span = pl.ds(n * size, size)
        sends.append(pltpu.make_async_copy(packed.at[span, :], out.at[span, :], out_sems.at[n]))
        sends[-1].start()
    for send in sends:
        send.wait()


def tile_kernel(got, out, wide, result, sems):
    peers = got.shape[0] // PEER_ROWS
    part = 8 * PEER_ROWS

    def widen(p, _):
        piece = pl.ds(pl.multiple_of(p * part, 16), part)
        wide[piece, :] = got[piece, :].astype(jnp.float32)
        return 0

    lax.fori_loop(0, peers // 8, widen, 0)

    def line_of_all(row):
        return wide[pl.ds(row, peers, stride=PEER_ROWS), :]

    lanes = lax.broadcasted_iota(jnp.int32, (peers, 128), 1)
    row_id = lanes.astype(jnp.float32)
    field, place = lanes // FIELD, lanes % FIELD
    pair_line = line_of_all(OWN_ROWS)
    slot_lines = [pair_line, pltpu.roll(pair_line, 64, 1), line_of_all(OWN_ROWS + 1)]
    stencil, here, over_next, over_own = [], [], [], []
    for line in slot_lines:
        table = jnp.zeros((peers, 128), jnp.float32)
        start = line[:, META : META + 1]
        for k in range(4):
            table = table + jnp.where(row_id == start + float(k), line[:, META + 2 + k : META + 3 + k], 0.0)
        stencil.append(table.T.astype(jnp.bfloat16))
        shift = jnp.broadcast_to(line[:, META + 1 : META + 2], (peers, 128)).astype(jnp.int32)
        step = lanes - shift
        mask = jnp.where((step >= -1) & (step <= 126), 1.0, 0.0).astype(jnp.bfloat16)
        here.append(jnp.concatenate([mask, mask], axis=1))
        ahead = place - shift + 1
        local_e = ahead - FIELD
        is_next = (ahead >= 0) & (ahead <= 2)
        is_own = (local_e >= 0) & (local_e <= 2)
        column = jnp.where(is_own, local_e, jnp.where(is_next, ahead, 0))
        nexts, owns = [], []
        for h in range(2):
            picked = jnp.take_along_axis(line, column + OVER * (field + 8 * h), axis=1)
            nexts.append(jnp.where(is_next, picked, 0.0))
            owns.append(jnp.where(is_own, picked, 0.0))
        over_next.append(jnp.concatenate(nexts, axis=1).astype(jnp.bfloat16))
        over_own.append(jnp.concatenate(owns, axis=1).astype(jnp.bfloat16))
    columns = jnp.concatenate(stencil, axis=1)
    here = jnp.concatenate(here, axis=0)

    def product(values):
        return jnp.dot(columns, values, preferred_element_type=jnp.float32)

    def later(x):
        return jnp.concatenate([x[128 - TL :], x[: 128 - TL]], axis=0)

    def earlier(x):
        return jnp.concatenate([x[TL:], x[:TL]], axis=0)

    onward = later(product(jnp.concatenate(over_next, axis=0)))
    local_over = product(jnp.concatenate(over_own, axis=0))
    lane = lax.broadcasted_iota(jnp.int32, (128, 128), 1)
    sends = []
    for pair in range(8):
        values = []
        for j in range(CAP):
            cols = [line_of_all(j * SLOT_ROWS + 2 * pair + e).astype(jnp.bfloat16) for e in range(2)]
            values.append(jnp.concatenate(cols, axis=1))
        values = jnp.concatenate(values, axis=0)
        staying = values * here
        total = product(staying)
        moving = product(values - staying)
        for e in range(2):
            fl = 2 * pair + e
            h, i = fl // 8, fl % 8
            ahead = pltpu.roll(onward[:, 128 * h : 128 * h + 128], (128 - FIELD * i) % 128, 1)
            behind = pltpu.roll(local_over[:, 128 * h : 128 * h + 128], (256 - FIELD - FIELD * i) % 128, 1)
            around = jnp.where(lane < FIELD, ahead, jnp.where(lane >= 128 - FIELD, behind, 0.0))
            part_moving = moving[:, 128 * e : 128 * e + 128]
            around = around + jnp.where(lane < 64, later(part_moving), earlier(part_moving))
            spot = (fl % 4, fl // 4)
            result[spot] = total[:, 128 * e : 128 * e + 128] + around
            sends.append(pltpu.make_async_copy(result.at[spot], out.at[spot], sems.at[fl]))
            sends[-1].start()
    for send in sends:
        send.wait()


def local(increments, band, tile_index, lat_offset, lon_shift, lat_frac, lon_frac):
    rows = increments.shape[0]
    n_lat = lax.axis_size("lat")
    peers = 4 * n_lat
    hbm = pl.BlockSpec(memory_space=pltpu.HBM)
    vmem = pl.BlockSpec(memory_space=pltpu.VMEM)
    whole = (peers * PEER_ROWS, 128)
    roomy = (peers * PEER_ROWS + SPARE, 128)
    send = pl.pallas_call(
        source_kernel,
        out_shape=jax.ShapeDtypeStruct(whole, jnp.bfloat16),
        in_specs=[hbm] * 7,
        out_specs=hbm,
        scratch_shapes=[pltpu.SMEM((rows,), jnp.int32)] * 4
        + [pltpu.SMEM((rows,), jnp.float32), pltpu.SMEM((n_lat,), jnp.int32)]
        + [pltpu.SMEM((rows,), jnp.int32)]
        + [
            pltpu.VMEM(increments.shape, jnp.bfloat16),
            pltpu.VMEM((rows, 128), jnp.float32),
            pltpu.VMEM((4, rows, 128), jnp.float32),
            pltpu.VMEM(roomy, jnp.float32),
            pltpu.VMEM(whole, jnp.bfloat16),
            pltpu.VMEM((rows * PITCH + SPARE, 128), jnp.float32),
            pltpu.VMEM((rows, 128), jnp.float32),
            pltpu.VMEM((8, rows, 128), jnp.float32),
            pltpu.VMEM((CAP, peers, 128), jnp.float32),
            pltpu.SemaphoreType.DMA((7,)),
            pltpu.SemaphoreType.DMA((OUT_PARTS,)),
        ],
        compiler_params=pltpu.CompilerParams(vmem_limit_bytes=60 << 20),
        name="lon_slots",
    )(band.reshape(rows), tile_index, lat_offset, lon_shift, lat_frac, increments, lon_frac)
    fine = (peers * PEER_ROWS // 2, 2, 128)
    got = lax.all_to_all(send.reshape(fine), ("lat", "grp"), 0, 0, tiled=True)
    return pl.pallas_call(
        tile_kernel,
        out_shape=jax.ShapeDtypeStruct((4, 4, 128, 128), jnp.float32),
        in_specs=[vmem],
        out_specs=hbm,
        scratch_shapes=[
            pltpu.VMEM(roomy, jnp.float32),
            pltpu.VMEM((4, 4, 128, 128), jnp.float32),
            pltpu.SemaphoreType.DMA((SLOT_ROWS,)),
        ],
        compiler_params=pltpu.CompilerParams(vmem_limit_bytes=40 << 20),
        name="tile_sums",
    )(got.reshape(whole))


def solution(mesh):
    in_specs = (
        P(("lat", "grp"), None, None, None),
        P(("lat", "grp"), None),
        P(("lat", "grp")),
        P(("lat", "grp")),
        P(("lat", "grp")),
        P(("lat", "grp")),
        P(("lat", "grp"), None),
    )
    out_specs = P("grp", None, "lat", None)
    return jax.shard_map(local, mesh=mesh, in_specs=in_specs, out_specs=out_specs, check_vma=False)
```

```python
import jax
import jax.numpy as jnp
from jax import lax
from jax.experimental import pallas as pl
from jax.experimental.pallas import tpu as pltpu
from jax.sharding import PartitionSpec as P

TL = 16
CAP = 3
SLOT_ROWS = 16
OWN_ROWS = CAP * SLOT_ROWS
PEER_ROWS = OWN_ROWS + 2
OVER = 3
META = OVER * SLOT_ROWS
FIELD = 16
PITCH = 65
OUT_PARTS = 8
SPARE = 72


def lagrange(fraction):
    return [
        -fraction * (fraction - 1.0) * (fraction - 2.0) / 6.0,
        (fraction + 1.0) * (fraction - 1.0) * (fraction - 2.0) / 2.0,
        -(fraction + 1.0) * fraction * (fraction - 2.0) / 2.0,
        (fraction + 1.0) * fraction * (fraction - 1.0) / 6.0,
    ]


def rounded(x):
    return x.astype(jnp.bfloat16).astype(jnp.float32)


def source_kernel(
    band_hbm, tile_hbm, offset_hbm, shift_hbm, lat_hbm, inc_hbm, lon_hbm, out,
    band, tile_index, lat_offset, lon_shift, lat_frac, count, slot_of,
    inc, lon_frac, weights, stage, packed, edges, meta_lines, lines, rests, sems, out_sems,
):
    rows = inc.shape[0]
    bands = count.shape[0]
    pairs = (
        (band_hbm, band), (tile_hbm, tile_index), (offset_hbm, lat_offset), (shift_hbm, lon_shift),
        (lat_hbm, lat_frac),
    )
    pairs = ((inc_hbm, inc), (lon_hbm, lon_frac)) + pairs
    copies = [pltpu.make_async_copy(src, dst, sems.at[i]) for i, (src, dst) in enumerate(pairs)]
    for copy in copies:
        copy.start()

    lane = lax.broadcasted_iota(jnp.int32, (8, 128), 1)
    sub = lax.broadcasted_iota(jnp.int32, (8, 128), 0)
    zero = jnp.zeros((8, 128), jnp.float32)
    part = out.shape[0] // (bands // 2)

    def clear(i, _):
        stage[pl.ds(pl.multiple_of(i * part, 8), part), :] = jnp.zeros((part, 128), jnp.float32)
        count[2 * i] = 0
        count[2 * i + 1] = 0
        return 0

    lax.fori_loop(0, bands // 2, clear, 0)
    rests[...] = jnp.zeros(rests.shape, jnp.float32)
    copies[1].wait()

    for m, w in enumerate(lagrange(lon_frac[...])):
        weights[m] = rounded(w)

    for copy in copies[2:]:
        copy.wait()
    copies[0].wait()

    def one_row(r, _):
        b = band[r]
        slot = count[b]
        count[b] = slot + 1
        slot_of[r] = slot
        peer_row = b * (4 * PEER_ROWS)
        shift = lon_shift[r]
        x = inc[r].astype(jnp.float32)
        pieces = [x[i // 2, 8 * (i % 2) : 8 * (i % 2) + 8] for i in range(8)]
        own = [None] * 8
        over = [None] * 8
        for m in range(4):
            move = (shift + (m - 1 + 128)) & 127
            w = jnp.broadcast_to(weights[m, pl.ds(r, 1), :], (8, 128))
            w = pltpu.roll(w, move, 1)
            inside = ((lane - shift - (m - 1)) & 127) < 128 - m
            own_w = jnp.where(inside, w, 0.0)
            over_w = jnp.where(inside, 0.0, w)
            for i in range(8):
                moved = pltpu.roll(pieces[i], move, 1)
                own[i] = own_w * moved if m == 0 else own[i] + own_w * moved
                if m > 0:
                    over[i] = over_w * moved if m == 1 else over[i] + over_w * moved
        at = peer_row + slot * SLOT_ROWS
        for i in range(8):
            f, h = i // 2, i % 2
            low = pl.ds(at + 2 * h * PEER_ROWS + 4 * f, 8)
            pltpu.store(stage.at[low, :], own[i], mask=sub < 4)
            high = pl.ds(at + (2 * h + 1) * PEER_ROWS + 4 * f - 4, 8)
            pltpu.store(stage.at[high, :], own[i], mask=sub >= 4)
            edges[pl.ds(r * PITCH + 8 * i, 8), :] = over[i]
        start = (tile_index[r] * TL + lat_offset[r]).astype(jnp.float32)
        meta = jnp.where(lane == META, start, jnp.where(lane == META + 1, shift.astype(jnp.float32), 0.0))
        meta = jnp.where(lane > META + 1, lat_frac[r], meta)
        meta_lines[pl.ds(r, 1), :] = meta[0:1]
        return 0

    lax.fori_loop(0, rows, one_row, 0, unroll=16)

    def pack(n, _):
        rows_here = pl.ds(pl.multiple_of(8 * n, 8), 8)
        meta = meta_lines[rows_here, :]
        shift = jnp.broadcast_to(meta[:, META + 1 : META + 2], (8, 128)).astype(jnp.int32)
        origin = (shift + 127 + lane % OVER) & 127
        for k, w in enumerate(lagrange(meta)):
            meta = jnp.where(lane == META + 2 + k, w, meta)
        meta = jnp.where((lane >= META) & (lane < META + 6), meta, 0.0)
        for g in range(4):
            whole = meta
            for fl in range(SLOT_ROWS):
                line = edges[pl.ds(n * (8 * PITCH) + (fl // 4) * 16 + 4 * g + fl % 4, 8, stride=PITCH), :]
                whole = jnp.where(lane // OVER == fl, jnp.take_along_axis(line, origin, axis=1), whole)
            lines[g, rows_here, :] = whole
            lines[4 + g, rows_here, :] = pltpu.roll(whole, 64, 1)
        return 0

    lax.fori_loop(0, rows // 8, pack, 0, unroll=2)

    def place(r, _):
        slot = slot_of[r]
        row = pl.ds(r, 1)
        peer = band[r] * 4
        side = jnp.where(slot == 1, 4, 0)
        for g in range(4):
            rests[slot, pl.ds(peer + g, 1), :] = lines[side + g, row, :]
        return 0

    lax.fori_loop(0, rows, place, 0, unroll=8)
    stage[pl.ds(OWN_ROWS, 4 * bands, stride=PEER_ROWS), :] = rests[0] + rests[1]
    stage[pl.ds(OWN_ROWS + 1, 4 * bands, stride=PEER_ROWS), :] = rests[2]

    size = out.shape[0] // OUT_PARTS
    sends = []
    for n in range(OUT_PARTS):

        def finish(i, _):
            piece = pl.ds(pl.multiple_of(n * size + i * part, 16), part)
            packed[piece, :] = stage[piece, :].astype(jnp.bfloat16)
            return 0

        lax.fori_loop(0, bands // (2 * OUT_PARTS), finish, 0)
        span = pl.ds(n * size, size)
        sends.append(pltpu.make_async_copy(packed.at[span, :], out.at[span, :], out_sems.at[n]))
        sends[-1].start()
    for send in sends:
        send.wait()


def tile_kernel(got, out, wide, result, sems):
    peers = got.shape[0] // PEER_ROWS
    part = 8 * PEER_ROWS

    def widen(p, _):
        piece = pl.ds(pl.multiple_of(p * part, 16), part)
        wide[piece, :] = got[piece, :].astype(jnp.float32)
        return 0

    lax.fori_loop(0, peers // 8, widen, 0, unroll=4)

    def line_of_all(row):
        return wide[pl.ds(row, peers, stride=PEER_ROWS), :]

    lanes = lax.broadcasted_iota(jnp.int32, (peers, 128), 1)
    field, place = lanes // FIELD, lanes % FIELD
    pair_line = line_of_all(OWN_ROWS)
    slot_lines = [pair_line, pltpu.roll(pair_line, 64, 1), line_of_all(OWN_ROWS + 1)]
    stencil, here, over_next, over_own = [], [], [], []
    for line in slot_lines:
        start = jnp.broadcast_to(line[:, META : META + 1], (peers, 128)).astype(jnp.int32)
        offset = lanes - start
        inside = (offset >= 0) & (offset < 4)
        pick = jnp.where(inside, offset, 0) + (META + 2)
        table = jnp.where(inside, jnp.take_along_axis(line, pick, axis=1), 0.0)
        stencil.append(table.T.astype(jnp.bfloat16))
        shift = jnp.broadcast_to(line[:, META + 1 : META + 2], (peers, 128)).astype(jnp.int32)
        step = lanes - shift
        mask = jnp.where((step >= -1) & (step <= 126), 1.0, 0.0).astype(jnp.bfloat16)
        here.append(jnp.concatenate([mask, mask], axis=1))
        ahead = place - shift + 1
        local_e = ahead - FIELD
        is_next = (ahead >= 0) & (ahead <= 2)
        is_own = (local_e >= 0) & (local_e <= 2)
        column = jnp.where(is_own, local_e, jnp.where(is_next, ahead, 0))
        nexts, owns = [], []
        for h in range(2):
            picked = jnp.take_along_axis(line, column + OVER * (field + 8 * h), axis=1)
            nexts.append(jnp.where(is_next, picked, 0.0))
            owns.append(jnp.where(is_own, picked, 0.0))
        over_next.append(jnp.concatenate(nexts, axis=1).astype(jnp.bfloat16))
        over_own.append(jnp.concatenate(owns, axis=1).astype(jnp.bfloat16))
    columns = jnp.concatenate(stencil, axis=1)
    here = jnp.concatenate(here, axis=0)

    def product(values):
        return jnp.dot(columns, values, preferred_element_type=jnp.float32)

    def later(x):
        return jnp.concatenate([x[128 - TL :], x[: 128 - TL]], axis=0)

    def earlier(x):
        return jnp.concatenate([x[TL:], x[:TL]], axis=0)

    onward = later(product(jnp.concatenate(over_next, axis=0)))
    local_over = product(jnp.concatenate(over_own, axis=0))
    lane = lax.broadcasted_iota(jnp.int32, (128, 128), 1)
    sends = []
    for pair in range(8):
        values = []
        for j in range(CAP):
            cols = [line_of_all(j * SLOT_ROWS + 2 * pair + e).astype(jnp.bfloat16) for e in range(2)]
            values.append(jnp.concatenate(cols, axis=1))
        values = jnp.concatenate(values, axis=0)
        staying = values * here
        total = product(staying)
        moving = product(values - staying)
        for e in range(2):
            fl = 2 * pair + e
            h, i = fl // 8, fl % 8
            ahead = pltpu.roll(onward[:, 128 * h : 128 * h + 128], (128 - FIELD * i) % 128, 1)
            behind = pltpu.roll(local_over[:, 128 * h : 128 * h + 128], (256 - FIELD - FIELD * i) % 128, 1)
            around = jnp.where(lane < FIELD, ahead, jnp.where(lane >= 128 - FIELD, behind, 0.0))
            part_moving = moving[:, 128 * e : 128 * e + 128]
            around = around + jnp.where(lane < 64, later(part_moving), earlier(part_moving))
            spot = (fl % 4, fl // 4)
            result[spot] = total[:, 128 * e : 128 * e + 128] + around
            sends.append(pltpu.make_async_copy(result.at[spot], out.at[spot], sems.at[fl]))
            sends[-1].start()
    for send in sends:
        send.wait()


def local(increments, band, tile_index, lat_offset, lon_shift, lat_frac, lon_frac):
    rows = increments.shape[0]
    n_lat = lax.axis_size("lat")
    peers = 4 * n_lat
    hbm = pl.BlockSpec(memory_space=pltpu.HBM)
    vmem = pl.BlockSpec(memory_space=pltpu.VMEM)
    whole = (peers * PEER_ROWS, 128)
    roomy = (peers * PEER_ROWS + SPARE, 128)
    send = pl.pallas_call(
        source_kernel,
        out_shape=jax.ShapeDtypeStruct(whole, jnp.bfloat16),
        in_specs=[hbm] * 7,
        out_specs=hbm,
        scratch_shapes=[pltpu.SMEM((rows,), jnp.int32)] * 4
        + [pltpu.SMEM((rows,), jnp.float32), pltpu.SMEM((n_lat,), jnp.int32)]
        + [pltpu.SMEM((rows,), jnp.int32)]
        + [
            pltpu.VMEM(increments.shape, jnp.bfloat16),
            pltpu.VMEM((rows, 128), jnp.float32),
            pltpu.VMEM((4, rows, 128), jnp.float32),
            pltpu.VMEM(roomy, jnp.float32),
            pltpu.VMEM(whole, jnp.bfloat16),
            pltpu.VMEM((rows * PITCH + SPARE, 128), jnp.float32),
            pltpu.VMEM((rows, 128), jnp.float32),
            pltpu.VMEM((8, rows, 128), jnp.float32),
            pltpu.VMEM((CAP, peers, 128), jnp.float32),
            pltpu.SemaphoreType.DMA((7,)),
            pltpu.SemaphoreType.DMA((OUT_PARTS,)),
        ],
        compiler_params=pltpu.CompilerParams(vmem_limit_bytes=60 << 20),
        name="lon_slots",
    )(band.reshape(rows), tile_index, lat_offset, lon_shift, lat_frac, increments, lon_frac)
    fine = (peers * PEER_ROWS // 2, 2, 128)
    got = lax.all_to_all(send.reshape(fine), ("lat", "grp"), 0, 0, tiled=True)
    return pl.pallas_call(
        tile_kernel,
        out_shape=jax.ShapeDtypeStruct((4, 4, 128, 128), jnp.float32),
        in_specs=[vmem],
        out_specs=hbm,
        scratch_shapes=[
            pltpu.VMEM(roomy, jnp.float32),
            pltpu.VMEM((4, 4, 128, 128), jnp.float32),
            pltpu.SemaphoreType.DMA((SLOT_ROWS,)),
        ],
        compiler_params=pltpu.CompilerParams(vmem_limit_bytes=40 << 20),
        name="tile_sums",
    )(got.reshape(whole))


def solution(mesh):
    in_specs = (
        P(("lat", "grp"), None, None, None),
        P(("lat", "grp"), None),
        P(("lat", "grp")),
        P(("lat", "grp")),
        P(("lat", "grp")),
        P(("lat", "grp")),
        P(("lat", "grp"), None),
    )
    out_specs = P("grp", None, "lat", None)
    return jax.shard_map(local, mesh=mesh, in_specs=in_specs, out_specs=out_specs, check_vma=False)
```

```python
import jax
import jax.numpy as jnp
from jax import lax
from jax.experimental import pallas as pl
from jax.experimental.pallas import tpu as pltpu
from jax.sharding import PartitionSpec as P

TL = 16
CAP = 3
SLOT_ROWS = 16
OWN_ROWS = CAP * SLOT_ROWS
PEER_ROWS = OWN_ROWS + 2
OVER = 3
META = OVER * SLOT_ROWS
FIELD = 16
PITCH = 65
SPARE = 72


def lagrange(fraction):
    return [
        -fraction * (fraction - 1.0) * (fraction - 2.0) / 6.0,
        (fraction + 1.0) * (fraction - 1.0) * (fraction - 2.0) / 2.0,
        -(fraction + 1.0) * fraction * (fraction - 2.0) / 2.0,
        (fraction + 1.0) * fraction * (fraction - 1.0) / 6.0,
    ]


def rounded(x):
    return x.astype(jnp.bfloat16).astype(jnp.float32)


def source_kernel(
    band_hbm, tile_hbm, offset_hbm, shift_hbm, lat_hbm, inc_hbm, lon_hbm, out,
    band, tile_index, lat_offset, lon_shift, lat_frac, count, slot_of,
    inc, lon_frac, weights, stage, edges, meta_lines, lines, rests, sems,
):
    rows = inc.shape[0]
    bands = count.shape[0]
    pairs = (
        (band_hbm, band), (tile_hbm, tile_index), (offset_hbm, lat_offset), (shift_hbm, lon_shift),
        (lat_hbm, lat_frac),
    )
    pairs = ((inc_hbm, inc), (lon_hbm, lon_frac)) + pairs
    copies = [pltpu.make_async_copy(src, dst, sems.at[i]) for i, (src, dst) in enumerate(pairs)]
    for copy in copies:
        copy.start()

    lane = lax.broadcasted_iota(jnp.int32, (8, 128), 1)
    sub = lax.broadcasted_iota(jnp.int32, (8, 128), 0)
    zero = jnp.zeros((8, 128), jnp.float32)
    part = out.shape[0] // (bands // 2)

    def clear(i, _):
        stage[pl.ds(pl.multiple_of(i * part, 8), part), :] = jnp.zeros((part, 128), jnp.float32)
        count[2 * i] = 0
        count[2 * i + 1] = 0
        return 0

    lax.fori_loop(0, bands // 2, clear, 0)
    rests[...] = jnp.zeros(rests.shape, jnp.float32)
    copies[1].wait()

    for m, w in enumerate(lagrange(lon_frac[...])):
        weights[m] = rounded(w)

    for copy in copies[2:]:
        copy.wait()
    copies[0].wait()

    def one_row(r, _):
        b = band[r]
        slot = count[b]
        count[b] = slot + 1
        slot_of[r] = slot
        peer_row = b * (4 * PEER_ROWS)
        shift = lon_shift[r]
        x = inc[r].astype(jnp.float32)
        pieces = [x[i // 2, 8 * (i % 2) : 8 * (i % 2) + 8] for i in range(8)]
        own = [None] * 8
        over = [None] * 8
        for m in range(4):
            move = (shift + (m - 1 + 128)) & 127
            w = jnp.broadcast_to(weights[m, pl.ds(r, 1), :], (8, 128))
            w = pltpu.roll(w, move, 1)
            inside = ((lane - shift - (m - 1)) & 127) < 128 - m
            own_w = jnp.where(inside, w, 0.0)
            over_w = jnp.where(inside, 0.0, w)
            for i in range(8):
                moved = pltpu.roll(pieces[i], move, 1)
                own[i] = own_w * moved if m == 0 else own[i] + own_w * moved
                if m > 0:
                    over[i] = over_w * moved if m == 1 else over[i] + over_w * moved
        at = peer_row + slot * SLOT_ROWS
        for i in range(8):
            f, h = i // 2, i % 2
            low = pl.ds(at + 2 * h * PEER_ROWS + 4 * f, 8)
            pltpu.store(stage.at[low, :], own[i], mask=sub < 4)
            high = pl.ds(at + (2 * h + 1) * PEER_ROWS + 4 * f - 4, 8)
            pltpu.store(stage.at[high, :], own[i], mask=sub >= 4)
            edges[pl.ds(r * PITCH + 8 * i, 8), :] = over[i]
        start = (tile_index[r] * TL + lat_offset[r]).astype(jnp.float32)
        meta = jnp.where(lane == META, start, jnp.where(lane == META + 1, shift.astype(jnp.float32), 0.0))
        meta = jnp.where(lane > META + 1, lat_frac[r], meta)
        meta_lines[pl.ds(r, 1), :] = meta[0:1]
        return 0

    lax.fori_loop(0, rows, one_row, 0, unroll=32)

    def pack(n, _):
        rows_here = pl.ds(pl.multiple_of(8 * n, 8), 8)
        meta = meta_lines[rows_here, :]
        shift = jnp.broadcast_to(meta[:, META + 1 : META + 2], (8, 128)).astype(jnp.int32)
        origin = (shift + 127 + lane % OVER) & 127
        for k, w in enumerate(lagrange(meta)):
            meta = jnp.where(lane == META + 2 + k, w, meta)
        meta = jnp.where((lane >= META) & (lane < META + 6), meta, 0.0)
        for g in range(4):
            whole = meta
            for fl in range(SLOT_ROWS):
                line = edges[pl.ds(n * (8 * PITCH) + (fl // 4) * 16 + 4 * g + fl % 4, 8, stride=PITCH), :]
                whole = jnp.where(lane // OVER == fl, jnp.take_along_axis(line, origin, axis=1), whole)
            lines[g, rows_here, :] = whole
            lines[4 + g, rows_here, :] = pltpu.roll(whole, 64, 1)
        return 0

    lax.fori_loop(0, rows // 8, pack, 0, unroll=2)

    def place(r, _):
        slot = slot_of[r]
        row = pl.ds(r, 1)
        peer = band[r] * 4
        side = jnp.where(slot == 1, 4, 0)
        for g in range(4):
            rests[slot, pl.ds(peer + g, 1), :] = lines[side + g, row, :]
        return 0

    lax.fori_loop(0, rows, place, 0, unroll=8)
    stage[pl.ds(OWN_ROWS, 4 * bands, stride=PEER_ROWS), :] = rests[0] + rests[1]
    stage[pl.ds(OWN_ROWS + 1, 4 * bands, stride=PEER_ROWS), :] = rests[2]

    def finish(i, _):
        piece = pl.ds(pl.multiple_of(i * part, 16), part)
        out[piece, :] = stage[piece, :].astype(jnp.bfloat16)
        return 0

    lax.fori_loop(0, bands // 2, finish, 0)


def tile_kernel(got, out, wide, result, sems):
    peers = got.shape[0] // PEER_ROWS
    part = 8 * PEER_ROWS

    def widen(p, _):
        piece = pl.ds(pl.multiple_of(p * part, 16), part)
        wide[piece, :] = got[piece, :].astype(jnp.float32)
        return 0

    lax.fori_loop(0, peers // 8, widen, 0, unroll=4)

    def line_of_all(row):
        return wide[pl.ds(row, peers, stride=PEER_ROWS), :]

    lanes = lax.broadcasted_iota(jnp.int32, (peers, 128), 1)
    field, place = lanes // FIELD, lanes % FIELD
    pair_line = line_of_all(OWN_ROWS)
    slot_lines = [pair_line, pltpu.roll(pair_line, 64, 1), line_of_all(OWN_ROWS + 1)]
    stencil, here, over_next, over_own = [], [], [], []
    for line in slot_lines:
        start = jnp.broadcast_to(line[:, META : META + 1], (peers, 128)).astype(jnp.int32)
        offset = lanes - start
        inside = (offset >= 0) & (offset < 4)
        pick = jnp.where(inside, offset, 0) + (META + 2)
        table = jnp.where(inside, jnp.take_along_axis(line, pick, axis=1), 0.0)
        stencil.append(table.T.astype(jnp.bfloat16))
        shift = jnp.broadcast_to(line[:, META + 1 : META + 2], (peers, 128)).astype(jnp.int32)
        step = lanes - shift
        mask = jnp.where((step >= -1) & (step <= 126), 1.0, 0.0).astype(jnp.bfloat16)
        here.append(jnp.concatenate([mask, mask], axis=1))
        ahead = place - shift + 1
        local_e = ahead - FIELD
        is_next = (ahead >= 0) & (ahead <= 2)
        is_own = (local_e >= 0) & (local_e <= 2)
        column = jnp.where(is_own, local_e, jnp.where(is_next, ahead, 0))
        nexts, owns = [], []
        for h in range(2):
            picked = jnp.take_along_axis(line, column + OVER * (field + 8 * h), axis=1)
            nexts.append(jnp.where(is_next, picked, 0.0))
            owns.append(jnp.where(is_own, picked, 0.0))
        over_next.append(jnp.concatenate(nexts, axis=1).astype(jnp.bfloat16))
        over_own.append(jnp.concatenate(owns, axis=1).astype(jnp.bfloat16))
    columns = jnp.concatenate(stencil, axis=1)
    here = jnp.concatenate(here, axis=0)

    def product(values):
        return jnp.dot(columns, values, preferred_element_type=jnp.float32)

    def later(x):
        return jnp.concatenate([x[128 - TL :], x[: 128 - TL]], axis=0)

    def earlier(x):
        return jnp.concatenate([x[TL:], x[:TL]], axis=0)

    onward = later(product(jnp.concatenate(over_next, axis=0)))
    local_over = product(jnp.concatenate(over_own, axis=0))
    lane = lax.broadcasted_iota(jnp.int32, (128, 128), 1)
    sends = []
    for pair in range(8):
        values = []
        for j in range(CAP):
            cols = [line_of_all(j * SLOT_ROWS + 2 * pair + e).astype(jnp.bfloat16) for e in range(2)]
            values.append(jnp.concatenate(cols, axis=1))
        values = jnp.concatenate(values, axis=0)
        staying = values * here
        total = product(staying)
        moving = product(values - staying)
        for e in range(2):
            fl = 2 * pair + e
            h, i = fl // 8, fl % 8
            ahead = pltpu.roll(onward[:, 128 * h : 128 * h + 128], (128 - FIELD * i) % 128, 1)
            behind = pltpu.roll(local_over[:, 128 * h : 128 * h + 128], (256 - FIELD - FIELD * i) % 128, 1)
            around = jnp.where(lane < FIELD, ahead, jnp.where(lane >= 128 - FIELD, behind, 0.0))
            part_moving = moving[:, 128 * e : 128 * e + 128]
            around = around + jnp.where(lane < 64, later(part_moving), earlier(part_moving))
            spot = (fl % 4, fl // 4)
            result[spot] = total[:, 128 * e : 128 * e + 128] + around
            sends.append(pltpu.make_async_copy(result.at[spot], out.at[spot], sems.at[fl]))
            sends[-1].start()
    for send in sends:
        send.wait()


def local(increments, band, tile_index, lat_offset, lon_shift, lat_frac, lon_frac):
    rows = increments.shape[0]
    n_lat = lax.axis_size("lat")
    peers = 4 * n_lat
    hbm = pl.BlockSpec(memory_space=pltpu.HBM)
    vmem = pl.BlockSpec(memory_space=pltpu.VMEM)
    whole = (peers * PEER_ROWS, 128)
    roomy = (peers * PEER_ROWS + SPARE, 128)
    operands = (band.reshape(rows), tile_index, lat_offset, lon_shift, lat_frac, increments, lon_frac)
    send = pl.pallas_call(
        source_kernel,
        out_shape=jax.ShapeDtypeStruct(whole, jnp.bfloat16),
        in_specs=[hbm] * 7,
        out_specs=vmem,
        scratch_shapes=[pltpu.SMEM((rows,), jnp.int32)] * 4
        + [pltpu.SMEM((rows,), jnp.float32), pltpu.SMEM((n_lat,), jnp.int32)]
        + [pltpu.SMEM((rows,), jnp.int32)]
        + [
            pltpu.VMEM(increments.shape, jnp.bfloat16),
            pltpu.VMEM((rows, 128), jnp.float32),
            pltpu.VMEM((4, rows, 128), jnp.float32),
            pltpu.VMEM(roomy, jnp.float32),
            pltpu.VMEM((rows * PITCH + SPARE, 128), jnp.float32),
            pltpu.VMEM((rows, 128), jnp.float32),
            pltpu.VMEM((8, rows, 128), jnp.float32),
            pltpu.VMEM((CAP, peers, 128), jnp.float32),
            pltpu.SemaphoreType.DMA((7,)),
        ],
        compiler_params=pltpu.CompilerParams(vmem_limit_bytes=32 << 20),
        name="lon_slots",
    )(*[pltpu.with_memory_space_constraint(operand, pltpu.HBM) for operand in operands])
    fine = (peers * PEER_ROWS // 2, 2, 128)
    got = lax.all_to_all(send.reshape(fine), ("lat", "grp"), 0, 0, tiled=True)
    return pl.pallas_call(
        tile_kernel,
        out_shape=jax.ShapeDtypeStruct((4, 4, 128, 128), jnp.float32),
        in_specs=[vmem],
        out_specs=hbm,
        scratch_shapes=[
            pltpu.VMEM(roomy, jnp.float32),
            pltpu.VMEM((4, 4, 128, 128), jnp.float32),
            pltpu.SemaphoreType.DMA((SLOT_ROWS,)),
        ],
        compiler_params=pltpu.CompilerParams(vmem_limit_bytes=40 << 20),
        name="tile_sums",
    )(got.reshape(whole))


def solution(mesh):
    in_specs = (
        P(("lat", "grp"), None, None, None),
        P(("lat", "grp"), None),
        P(("lat", "grp")),
        P(("lat", "grp")),
        P(("lat", "grp")),
        P(("lat", "grp")),
        P(("lat", "grp"), None),
    )
    out_specs = P("grp", None, "lat", None)
    return jax.shard_map(local, mesh=mesh, in_specs=in_specs, out_specs=out_specs, check_vma=False)
```

```python
import jax
import jax.numpy as jnp
from jax import lax
from jax.experimental import pallas as pl
from jax.experimental.pallas import tpu as pltpu
from jax.sharding import PartitionSpec as P

TL = 16
CAP = 3
SLOT_ROWS = 16
OWN_ROWS = CAP * SLOT_ROWS
PEER_ROWS = OWN_ROWS + 2
OVER = 3
META = OVER * SLOT_ROWS
FIELD = 16
PITCH = 65
SPARE = 72


def lagrange(fraction):
    return [
        -fraction * (fraction - 1.0) * (fraction - 2.0) / 6.0,
        (fraction + 1.0) * (fraction - 1.0) * (fraction - 2.0) / 2.0,
        -(fraction + 1.0) * fraction * (fraction - 2.0) / 2.0,
        (fraction + 1.0) * fraction * (fraction - 1.0) / 6.0,
    ]


def rounded(x):
    return x.astype(jnp.bfloat16).astype(jnp.float32)


def source_kernel(
    band_hbm, tile_hbm, offset_hbm, shift_hbm, lat_hbm, inc_hbm, lon_hbm, out,
    band, tile_index, lat_offset, lon_shift, lat_frac, count, slot_of,
    inc, lon_frac, weights, stage, edges, meta_lines, lines, rests, sems,
):
    rows = inc.shape[0]
    bands = count.shape[0]
    pairs = (
        (band_hbm, band), (tile_hbm, tile_index), (offset_hbm, lat_offset), (shift_hbm, lon_shift),
        (lat_hbm, lat_frac),
    )
    near = rows // 2
    pairs = (
        (inc_hbm.at[pl.ds(0, near)], inc.at[pl.ds(0, near)]), (lon_hbm, lon_frac),
        (inc_hbm.at[pl.ds(near, rows - near)], inc.at[pl.ds(near, rows - near)]),
    ) + pairs
    copies = [pltpu.make_async_copy(src, dst, sems.at[i]) for i, (src, dst) in enumerate(pairs)]
    for copy in copies:
        copy.start()

    lane = lax.broadcasted_iota(jnp.int32, (8, 128), 1)
    sub = lax.broadcasted_iota(jnp.int32, (8, 128), 0)
    zero = jnp.zeros((8, 128), jnp.float32)
    part = out.shape[0] // (bands // 2)

    def clear(i, _):
        stage[pl.ds(pl.multiple_of(i * part, 8), part), :] = jnp.zeros((part, 128), jnp.float32)
        count[2 * i] = 0
        count[2 * i + 1] = 0
        return 0

    lax.fori_loop(0, bands // 2, clear, 0, unroll=4)
    rests[...] = jnp.zeros(rests.shape, jnp.float32)
    copies[1].wait()

    for m, w in enumerate(lagrange(lon_frac[...])):
        weights[m] = rounded(w)

    for copy in copies[3:]:
        copy.wait()
    copies[0].wait()

    def one_row(r, _):
        b = band[r]
        slot = count[b]
        count[b] = slot + 1
        slot_of[r] = slot
        peer_row = b * (4 * PEER_ROWS)
        shift = lon_shift[r]
        x = inc[r].astype(jnp.float32)
        pieces = [x[i // 2, 8 * (i % 2) : 8 * (i % 2) + 8] for i in range(8)]
        own = [None] * 8
        over = [None] * 8
        for m in range(4):
            move = (shift + (m - 1 + 128)) & 127
            w = jnp.broadcast_to(weights[m, pl.ds(r, 1), :], (8, 128))
            w = pltpu.roll(w, move, 1)
            inside = ((lane - shift - (m - 1)) & 127) < 128 - m
            own_w = jnp.where(inside, w, 0.0)
            over_w = jnp.where(inside, 0.0, w)
            for i in range(8):
                moved = pltpu.roll(pieces[i], move, 1)
                own[i] = own_w * moved if m == 0 else own[i] + own_w * moved
                if m > 0:
                    over[i] = over_w * moved if m == 1 else over[i] + over_w * moved
        at = peer_row + slot * SLOT_ROWS
        for i in range(8):
            f, h = i // 2, i % 2
            low = pl.ds(at + 2 * h * PEER_ROWS + 4 * f, 8)
            pltpu.store(stage.at[low, :], own[i], mask=sub < 4)
            high = pl.ds(at + (2 * h + 1) * PEER_ROWS + 4 * f - 4, 8)
            pltpu.store(stage.at[high, :], own[i], mask=sub >= 4)
            edges[pl.ds(r * PITCH + 8 * i, 8), :] = over[i]
        start = (tile_index[r] * TL + lat_offset[r]).astype(jnp.float32)
        meta = jnp.where(lane == META, start, jnp.where(lane == META + 1, shift.astype(jnp.float32), 0.0))
        meta = jnp.where(lane > META + 1, lat_frac[r], meta)
        meta_lines[pl.ds(r, 1), :] = meta[0:1]
        return 0

    lax.fori_loop(0, near, one_row, 0, unroll=32)
    copies[2].wait()
    lax.fori_loop(near, rows, one_row, 0, unroll=32)

    def pack(n, _):
        rows_here = pl.ds(pl.multiple_of(8 * n, 8), 8)
        meta = meta_lines[rows_here, :]
        shift = jnp.broadcast_to(meta[:, META + 1 : META + 2], (8, 128)).astype(jnp.int32)
        origin = (shift + 127 + lane % OVER) & 127
        for k, w in enumerate(lagrange(meta)):
            meta = jnp.where(lane == META + 2 + k, w, meta)
        meta = jnp.where((lane >= META) & (lane < META + 6), meta, 0.0)
        for g in range(4):
            whole = meta
            for fl in range(SLOT_ROWS):
                line = edges[pl.ds(n * (8 * PITCH) + (fl // 4) * 16 + 4 * g + fl % 4, 8, stride=PITCH), :]
                whole = jnp.where(lane // OVER == fl, jnp.take_along_axis(line, origin, axis=1), whole)
            lines[g, rows_here, :] = whole
            lines[4 + g, rows_here, :] = pltpu.roll(whole, 64, 1)
        return 0

    lax.fori_loop(0, rows // 8, pack, 0, unroll=2)

    def place(r, _):
        slot = slot_of[r]
        row = pl.ds(r, 1)
        peer = band[r] * 4
        side = jnp.where(slot == 1, 4, 0)
        for g in range(4):
            rests[slot, pl.ds(peer + g, 1), :] = lines[side + g, row, :]
        return 0

    lax.fori_loop(0, rows, place, 0, unroll=8)
    stage[pl.ds(OWN_ROWS, 4 * bands, stride=PEER_ROWS), :] = rests[0] + rests[1]
    stage[pl.ds(OWN_ROWS + 1, 4 * bands, stride=PEER_ROWS), :] = rests[2]

    def finish(i, _):
        piece = pl.ds(pl.multiple_of(i * part, 16), part)
        out[piece, :] = stage[piece, :].astype(jnp.bfloat16)
        return 0

    lax.fori_loop(0, bands // 2, finish, 0, unroll=4)


def tile_kernel(got, out, wide, result, sems):
    peers = got.shape[0] // PEER_ROWS
    part = 8 * PEER_ROWS

    def widen(p, _):
        piece = pl.ds(pl.multiple_of(p * part, 16), part)
        wide[piece, :] = got[piece, :].astype(jnp.float32)
        return 0

    lax.fori_loop(0, peers // 8, widen, 0, unroll=8)

    def line_of_all(row):
        return wide[pl.ds(row, peers, stride=PEER_ROWS), :]

    lanes = lax.broadcasted_iota(jnp.int32, (peers, 128), 1)
    field, place = lanes // FIELD, lanes % FIELD
    pair_line = line_of_all(OWN_ROWS)
    slot_lines = [pair_line, pltpu.roll(pair_line, 64, 1), line_of_all(OWN_ROWS + 1)]
    stencil, here, over_next, over_own = [], [], [], []
    for line in slot_lines:
        start = jnp.broadcast_to(line[:, META : META + 1], (peers, 128)).astype(jnp.int32)
        offset = lanes - start
        inside = (offset >= 0) & (offset < 4)
        pick = jnp.where(inside, offset, 0) + (META + 2)
        table = jnp.where(inside, jnp.take_along_axis(line, pick, axis=1), 0.0)
        stencil.append(table.T.astype(jnp.bfloat16))
        shift = jnp.broadcast_to(line[:, META + 1 : META + 2], (peers, 128)).astype(jnp.int32)
        step = lanes - shift
        mask = jnp.where((step >= -1) & (step <= 126), 1.0, 0.0).astype(jnp.bfloat16)
        here.append(jnp.concatenate([mask, mask], axis=1))
        ahead = place - shift + 1
        local_e = ahead - FIELD
        is_next = (ahead >= 0) & (ahead <= 2)
        is_own = (local_e >= 0) & (local_e <= 2)
        column = jnp.where(is_own, local_e, jnp.where(is_next, ahead, 0))
        nexts, owns = [], []
        for h in range(2):
            picked = jnp.take_along_axis(line, column + OVER * (field + 8 * h), axis=1)
            nexts.append(jnp.where(is_next, picked, 0.0))
            owns.append(jnp.where(is_own, picked, 0.0))
        over_next.append(jnp.concatenate(nexts, axis=1).astype(jnp.bfloat16))
        over_own.append(jnp.concatenate(owns, axis=1).astype(jnp.bfloat16))
    columns = jnp.concatenate(stencil, axis=1)
    here = jnp.concatenate(here, axis=0)

    def product(values):
        return jnp.dot(columns, values, preferred_element_type=jnp.float32)

    def later(x):
        return jnp.concatenate([x[128 - TL :], x[: 128 - TL]], axis=0)

    def earlier(x):
        return jnp.concatenate([x[TL:], x[:TL]], axis=0)

    onward = later(product(jnp.concatenate(over_next, axis=0)))
    local_over = product(jnp.concatenate(over_own, axis=0))
    lane = lax.broadcasted_iota(jnp.int32, (128, 128), 1)
    sends = []
    for pair in range(8):
        values = []
        for j in range(CAP):
            cols = [line_of_all(j * SLOT_ROWS + 2 * pair + e).astype(jnp.bfloat16) for e in range(2)]
            values.append(jnp.concatenate(cols, axis=1))
        values = jnp.concatenate(values, axis=0)
        staying = values * here
        total = product(staying)
        moving = product(values - staying)
        for e in range(2):
            fl = 2 * pair + e
            h, i = fl // 8, fl % 8
            ahead = pltpu.roll(onward[:, 128 * h : 128 * h + 128], (128 - FIELD * i) % 128, 1)
            behind = pltpu.roll(local_over[:, 128 * h : 128 * h + 128], (256 - FIELD - FIELD * i) % 128, 1)
            around = jnp.where(lane < FIELD, ahead, jnp.where(lane >= 128 - FIELD, behind, 0.0))
            part_moving = moving[:, 128 * e : 128 * e + 128]
            around = around + jnp.where(lane < 64, later(part_moving), earlier(part_moving))
            spot = (fl % 4, fl // 4)
            result[spot] = total[:, 128 * e : 128 * e + 128] + around
            sends.append(pltpu.make_async_copy(result.at[spot], out.at[spot], sems.at[fl]))
            sends[-1].start()
    for send in sends:
        send.wait()


def local(increments, band, tile_index, lat_offset, lon_shift, lat_frac, lon_frac):
    rows = increments.shape[0]
    n_lat = lax.axis_size("lat")
    peers = 4 * n_lat
    hbm = pl.BlockSpec(memory_space=pltpu.HBM)
    vmem = pl.BlockSpec(memory_space=pltpu.VMEM)
    whole = (peers * PEER_ROWS, 128)
    roomy = (peers * PEER_ROWS + SPARE, 128)
    operands = (band.reshape(rows), tile_index, lat_offset, lon_shift, lat_frac, increments, lon_frac)
    send = pl.pallas_call(
        source_kernel,
        out_shape=jax.ShapeDtypeStruct(whole, jnp.bfloat16),
        in_specs=[hbm] * 7,
        out_specs=vmem,
        scratch_shapes=[pltpu.SMEM((rows,), jnp.int32)] * 4
        + [pltpu.SMEM((rows,), jnp.float32), pltpu.SMEM((n_lat,), jnp.int32)]
        + [pltpu.SMEM((rows,), jnp.int32)]
        + [
            pltpu.VMEM(increments.shape, jnp.bfloat16),
            pltpu.VMEM((rows, 128), jnp.float32),
            pltpu.VMEM((4, rows, 128), jnp.float32),
            pltpu.VMEM(roomy, jnp.float32),
            pltpu.VMEM((rows * PITCH + SPARE, 128), jnp.float32),
            pltpu.VMEM((rows, 128), jnp.float32),
            pltpu.VMEM((8, rows, 128), jnp.float32),
            pltpu.VMEM((CAP, peers, 128), jnp.float32),
            pltpu.SemaphoreType.DMA((8,)),
        ],
        compiler_params=pltpu.CompilerParams(vmem_limit_bytes=32 << 20),
        name="lon_slots",
    )(*[pltpu.with_memory_space_constraint(operand, pltpu.HBM) for operand in operands])
    fine = (peers * PEER_ROWS // 2, 2, 128)
    got = lax.all_to_all(send.reshape(fine), ("lat", "grp"), 0, 0, tiled=True)
    return pl.pallas_call(
        tile_kernel,
        out_shape=jax.ShapeDtypeStruct((4, 4, 128, 128), jnp.float32),
        in_specs=[vmem],
        out_specs=hbm,
        scratch_shapes=[
            pltpu.VMEM(roomy, jnp.float32),
            pltpu.VMEM((4, 4, 128, 128), jnp.float32),
            pltpu.SemaphoreType.DMA((SLOT_ROWS,)),
        ],
        compiler_params=pltpu.CompilerParams(vmem_limit_bytes=40 << 20),
        name="tile_sums",
    )(got.reshape(whole))


def solution(mesh):
    in_specs = (
        P(("lat", "grp"), None, None, None),
        P(("lat", "grp"), None),
        P(("lat", "grp")),
        P(("lat", "grp")),
        P(("lat", "grp")),
        P(("lat", "grp")),
        P(("lat", "grp"), None),
    )
    out_specs = P("grp", None, "lat", None)
    return jax.shard_map(local, mesh=mesh, in_specs=in_specs, out_specs=out_specs, check_vma=False)
```
